768 devices in a mesh: morton: 192 (over y, z, core), sub: 4 (over x).
Axes of the slice: x: 4, y: 8, z: 12, core: 2. Of those that a mesh axis runs over, the one named last changes fastest.
Arguments:
- direction: float32 [49152, 3, 512], P(('morton', 'sub')), may hold values from -6 to 6
- jacobian: float32 [49152, 512], P(('morton', 'sub')), may hold values from 0.8 to 1.25
- shear_modulus: float32 [49152], P(('morton', 'sub')), may hold values from 0.5 to 2
- lame_modulus: float32 [49152], P(('morton', 'sub')), may hold values from 0.4 to 1.6
- refine_level: int32 [49152], P(('morton', 'sub')), may hold values from 1 to 2, as said below
- live_flag: int32 [49152], P(('morton', 'sub')), may hold values from 0 to 1, as said below
- neighbor: int32 [49152, 6], P(('morton', 'sub')), may hold values from 0 to 49151, as said below
- face_kind: int32 [49152, 6], P(('morton', 'sub')), may hold values from 0 to 2, as said below
- face_quadrant: int32 [49152, 6], P(('morton', 'sub')), may hold values from 0 to 3
Outputs:
- hessian_product: float32 [49152, 3, 512], P(('morton', 'sub'))
The draws below stay inside these ranges and needn't reach their ends.
Inputs may be any that keep to these rules, and one draw needn't show every extreme that they name: `neighbor`: each entry names a live block whose device's index along morton differs from the block's own by at most one. The 384 entries of one device's blocks name blocks of any single device at most 64 times; the devices of the first Morton range reach that. `live_flag`: A device's live blocks come first among its 64 blocks; each device has at least a quarter of its blocks live, and some devices, the last one among them, have all live. The grid spacing of a block is 2 ** (-refine_level) relative to level 0. `face_kind`: 2 exactly where the neighbour's refine_level is one less than the block's own, 1 where the two are equal, 0 where the neighbour is finer.
All inputs are finite; a program needn't handle non-finite values.
Results may differ from the reference program's by a relative error of at most 0.00005.
Values sent between devices are 32-bit elements; how exact they have to be, the bound alone decides.
A program may use at most 32 MiB of HBM per device.

```python
import math
import jax
import jax.numpy as jnp
from jax import lax

BLK = 64
NODES = 512
NB = 49152
N_SUB = 4


def live_counts(key):
    devices_all = NB // BLK
    first, second = jax.random.split(jax.random.fold_in(key, 101))
    counts = jax.random.randint(first, (devices_all,), max(1, BLK // 4), BLK + 1)
    chosen = jax.random.randint(second, (), 0, devices_all)
    counts = counts.at[chosen].set(BLK)
    counts = counts.at[devices_all - 1].set(BLK)
    return counts.astype(jnp.int32)


def neighbor_table(key):
    counts = live_counts(key)
    first, second = jax.random.split(jax.random.fold_in(key, 111))
    devices_all = NB // BLK
    ranges = devices_all // N_SUB
    slots = 6 * BLK
    scores = jax.random.randint(first, (devices_all, slots), 0, 2 ** 20) * slots + jnp.arange(slots, dtype=jnp.int32)[None, :]
    ranked = jnp.argsort(jnp.argsort(scores, axis=1), axis=1).astype(jnp.int32)
    picked = ranked % (3 * N_SUB)
    device = jnp.arange(devices_all, dtype=jnp.int32)[:, None]
    target_morton = jnp.clip(device // N_SUB + picked // N_SUB - 1, 0, ranges - 1)
    target = target_morton * N_SUB + picked % N_SUB
    local_pos = jax.random.randint(second, (devices_all, slots), 0, BLK) % counts[target]
    return (target * BLK + local_pos).reshape(NB, 6).astype(jnp.int32)


def level_table(key):
    return jax.random.randint(jax.random.fold_in(key, 131), (NB,), 1, 3).astype(jnp.int32)


def draw_live_flag(key, part):
    counts = live_counts(key)
    positions = jnp.arange(NB, dtype=jnp.int32)
    return (positions % BLK < counts[positions // BLK]).astype(jnp.int32)


def draw_neighbor(key, part):
    table = neighbor_table(key)
    return table


def draw_refine_level(key, part):
    levels = level_table(key)
    return levels


def draw_face_kind(key, part):
    table = neighbor_table(key)
    levels = level_table(key)
    across = levels[table]
    own_level = levels[:, None]
    return jnp.where(across == own_level - 1, 2, jnp.where(across == own_level, 1, 0)).astype(jnp.int32)


def plant(values, own_key, low, high):
    longest = values.shape.index(max(values.shape))
    spots = []
    for shift in (0, 1):
        where = [jax.random.randint(jax.random.fold_in(own_key, axis), (), 0, length) for axis, length in enumerate(values.shape)]
        where[longest] = (where[longest] + shift) % values.shape[longest]
        spots.append(tuple(where))
    return values.at[spots[0]].set(low).at[spots[1]].set(high)


def steps_of(stream_key, extent, cuts, low, top_value):
    level, own = 1.0, jax.random.fold_in(stream_key, 6)
    for dim, shards_of in cuts:
        draws = jnp.exp(jax.random.uniform(jax.random.fold_in(own, dim), (shards_of,), jnp.float32, low / len(cuts), top_value / len(cuts)))
        level = level * jnp.repeat(draws, extent[dim] // shards_of).reshape([-1 if axis == dim else 1 for axis in range(len(extent))])
    return level


def centred(stream_key, dims, scale, most, shards=(), held_as=jnp.bfloat16):
    values = jax.random.normal(stream_key, dims, jnp.float32) * scale
    if len(shards) > 0:
        values = steps_of(stream_key, dims, shards, -0.22, 0.18) * values
    return jnp.clip(values, min=-most, max=most).astype(held_as)


def setup_inputs(seed: int = 0) -> dict:
    seeds = jax.random.split(jax.random.key(seed), 10)
    direction = centred(seeds[0], (NB, 3, NODES), 1.0, 6.0, ((0, 768),), jnp.float32)
    jacobian = jnp.clip(jnp.exp(math.log(1.25) - 0.4462871 * jax.random.uniform(seeds[1], (NB, NODES), jnp.float32) ** steps_of(seeds[1], (NB, NODES), ((0, 768),), -0.2, 0.2)), 0.8, 1.25)
    shear_modulus = jnp.clip(jnp.exp(math.log(2.0) - 1.3862944 * jax.random.uniform(seeds[2], (NB,), jnp.float32) ** steps_of(seeds[2], (NB,), ((0, 768),), -0.2, 0.2)), 0.5, 2.0)
    lame_modulus = jnp.clip(jnp.exp(math.log(1.6) - 1.3862944 * jax.random.uniform(seeds[3], (NB,), jnp.float32) ** steps_of(seeds[3], (NB,), ((0, 768),), -0.2, 0.2)), 0.4, 1.6)
    refine_level = draw_refine_level(jax.random.fold_in(seeds[9], 71), 0)
    live_flag = draw_live_flag(jax.random.fold_in(seeds[9], 71), 0)
    neighbor = draw_neighbor(jax.random.fold_in(seeds[9], 71), 0)
    face_kind = draw_face_kind(jax.random.fold_in(seeds[9], 71), 0)
    face_quadrant = plant(jax.random.randint(seeds[8], (NB, 6), 0, 4), jax.random.fold_in(seeds[8], 1), 0, 3).astype(jnp.int32)
    return dict(direction=direction, jacobian=jacobian, shear_modulus=shear_modulus, lame_modulus=lame_modulus, refine_level=refine_level, live_flag=live_flag, neighbor=neighbor, face_kind=face_kind, face_quadrant=face_quadrant)


def face_layers(nodal):
    blocks = nodal.shape[0]
    cube = nodal.reshape(blocks, 3, 8, 8, 8)
    layer_list = [cube[:, :, 0], cube[:, :, 7], cube[:, :, :, 0], cube[:, :, :, 7], cube[:, :, :, :, 0], cube[:, :, :, :, 7]]
    return jnp.stack([layer.reshape(blocks, 3, 64) for layer in layer_list], axis=1)

def prolong_tables():
    fine = jnp.arange(8, dtype=jnp.int32)
    coarse = jnp.arange(8, dtype=jnp.int32)
    halves = []
    for upper_part in range(2):
        doubled = 7 * upper_part + fine
        lower_hit = ((doubled // 2)[:, None] == coarse[None, :]).astype(jnp.float32)
        upper_hit = (((doubled + 1) // 2)[:, None] == coarse[None, :]).astype(jnp.float32)
        halves.append(0.5 * lower_hit + 0.5 * upper_hit)
    return jnp.stack([jnp.kron(halves[quad // 2], halves[quad % 2]) for quad in range(4)])

def fill_ghost(raw_ghost, face_kind, face_quadrant):
    spread = jnp.einsum('xpq,bfcq->xbfcp', prolong_tables(), raw_ghost, precision=lax.Precision.HIGHEST)
    picks = jnp.arange(4, dtype=jnp.int32)[:, None, None, None, None] == face_quadrant[None, :, :, None, None]
    hanging = lax.optimization_barrier(jnp.sum(jnp.where(picks, spread, jnp.zeros_like(spread)), axis=0))
    kind_mask = face_kind[:, :, None, None]
    return jnp.where(kind_mask == 1, raw_ghost, jnp.where(kind_mask == 2, hanging, jnp.zeros_like(raw_ghost)))

def gradient(nodal, ghost_vals, block_scale):
    blocks = nodal.shape[0]
    cube = nodal.reshape(blocks, 3, 8, 8, 8)
    pieces = []
    for axis_id in range(3):
        low_side = jnp.expand_dims(ghost_vals[:, 2 * axis_id].reshape(blocks, 3, 8, 8), 2 + axis_id)
        high_side = jnp.expand_dims(ghost_vals[:, 2 * axis_id + 1].reshape(blocks, 3, 8, 8), 2 + axis_id)
        padded = jnp.concatenate([low_side, cube, high_side], axis=2 + axis_id)
        ahead = lax.slice_in_dim(padded, 2, 10, axis=2 + axis_id)
        behind = lax.slice_in_dim(padded, 0, 8, axis=2 + axis_id)
        pieces.append((0.5 * (ahead - behind)).reshape(blocks, 3, 512))
    strain = jnp.stack(pieces, axis=2)
    return strain * block_scale[:, None, None, None]

def stress_of(strain, jacobian, shear_modulus, lame_modulus):
    volume_change = strain[:, 0, 0] + strain[:, 1, 1] + strain[:, 2, 2]
    shear_mod = shear_modulus[:, None] - lame_modulus[:, None] * jnp.log(jacobian)
    symmetric = strain + jnp.swapaxes(strain, 1, 2)
    identity = jnp.eye(3, dtype=jnp.float32)
    return lame_modulus[:, None, None, None] * volume_change[:, None, None, :] * identity[None, :, :, None] + shear_mod[:, None, None, :] * symmetric

def reference(direction, jacobian, shear_modulus, lame_modulus, refine_level, live_flag, neighbor, face_kind, face_quadrant):
    block_scale = 0.5 * jnp.exp2(refine_level.astype(jnp.float32))
    live_mask = live_flag.astype(jnp.float32)
    opposite = jnp.array([1, 0, 3, 2, 5, 4], dtype=jnp.int32)

    def tangent(nodal):
        masked = nodal * live_mask[:, None, None]
        face_vals = face_layers(masked)
        raw_ghost = face_vals[neighbor, opposite[None, :]]
        ghost_vals = fill_ghost(raw_ghost, face_kind, face_quadrant)
        return gradient(masked, ghost_vals, block_scale)
    strain, pullback = jax.vjp(tangent, direction)
    stress = stress_of(strain, jacobian, shear_modulus, lame_modulus)
    result, = pullback(stress)
    return result
```

```python
import functools

import jax
import jax.numpy as jnp
import numpy as np
from jax import lax
from jax.experimental import pallas as pl
from jax.experimental.pallas import tpu as pltpu
from jax.sharding import PartitionSpec as P

BLOCKS = 64
ROWS = 6 * BLOCKS
PEERS = 12
SLOTS = PEERS * BLOCKS
SELF = 4
F32 = jnp.float32
BF16 = jnp.bfloat16
MESH = pl.DeviceIdType.MESH
GROUPS = ((2, 6, 10), (1, 3, 5, 7, 9, 11), (0, 8, 4))
ORDER = tuple(p for group in GROUPS for p in group)


def tables():
    node = np.arange(512)
    coords = (node // 64, (node // 8) % 8, node % 8)
    pick = np.zeros((512, 6, 64), np.float32)
    for face in range(6):
        axis = face // 2
        others = [coords[a] for a in range(3) if a != axis]
        for n in np.nonzero(coords[axis] == 7 * (face % 2))[0]:
            pick[n, face, others[0][n] * 8 + others[1][n]] = 1
    halves = np.zeros((2, 8, 8), np.float32)
    for u in range(2):
        for i in range(8):
            halves[u, i, (7 * u + i) // 2] += 0.5
            halves[u, i, (7 * u + i + 1) // 2] += 0.5
    fill = np.zeros((128, 512), np.float32)
    unfill = np.zeros((128, 512), np.float32)
    for q in range(4):
        spread = np.kron(halves[q // 2], halves[q % 2])
        for half in range(2):
            lanes = slice(64 * half, 64 * half + 64)
            cols = slice(128 * q + 64 * half, 128 * q + 64 * half + 64)
            fill[lanes, cols] = spread.T
            unfill[lanes, cols] = spread
    twice = np.concatenate([pick, pick], axis=2).reshape(512, 768)
    inject = pick.reshape(512, ROWS).T
    before = np.triu(np.ones((ROWS, ROWS), np.float32), 1)
    return [jnp.asarray(t, BF16) for t in (twice, inject, fill, unfill, before)]


def split(values):
    high = values.astype(BF16)
    low = (values - high.astype(F32)).astype(BF16)
    return high, low


def dot(a, b):
    return jnp.dot(a, b, preferred_element_type=F32)


def lane_iota(shape):
    return lax.broadcasted_iota(jnp.int32, shape, len(shape) - 1)


def kernel(
    ranges,
    x_hbm, jac_hbm, mu_hbm, lam_hbm, level_hbm, live_hbm, nb_hbm, kind_hbm, quad_hbm,
    twice_hbm, inject_hbm, fill_hbm, unfill_hbm, before_hbm,
    out_ref,
    x, jac, mu, lam, level, live, nb, kind, quad,
    twice, inject, fill, unfill, before,
    tile_s, code_b, coef, table, sel, sel_t, place, place_t, lists, lists_in,
    fsend, frecv, asend, arecv, landed_rows, sym, inj, back,
    in_sem, list_ssem, list_rsem, f_ssem, f_rsem, a_ssem, a_rsem,
):
    me_m = lax.axis_index("morton")
    me_x = lax.axis_index("sub")

    def device(p):
        dm, dx = p // 4 - 1, p % 4
        return (lax.rem(me_m + (dm + ranges), ranges), lax.rem(me_x + dx, 4))

    def mirror(p):
        return (2 - p // 4) * 4 + (4 - p % 4) % 4

    def remote(p, src, dst, ssem, rsem):
        return pltpu.make_async_remote_copy(
            src_ref=src, dst_ref=dst.at[mirror(p)], send_sem=ssem.at[p], recv_sem=rsem.at[mirror(p)],
            device_id=device(p), device_id_type=MESH,
        )

    def arrival(p, dst, ssem, rsem):
        return pltpu.make_async_remote_copy(
            src_ref=dst.at[p], dst_ref=dst.at[p], send_sem=ssem.at[p], recv_sem=rsem.at[p],
            device_id=device(p), device_id_type=MESH,
        )

    loads = [
        pltpu.make_async_copy(src, dst, in_sem.at[i])
        for i, (src, dst) in enumerate(
            (
                (nb_hbm, nb), (before_hbm, before), (kind_hbm, kind), (quad_hbm, quad),
                (live_hbm, live), (mu_hbm, mu), (lam_hbm, lam), (level_hbm, level),
                (x_hbm, x), (twice_hbm, twice), (jac_hbm, jac), (inject_hbm, inject),
                (fill_hbm, fill), (unfill_hbm, unfill),
            )
        )
    ]
    for load in loads:
        load.start()
    barrier = pltpu.get_barrier_semaphore()
    for p in ORDER:
        if p != SELF:
            pl.semaphore_signal(barrier, inc=1, device_id=device(p), device_id_type=MESH)

    low_half = lane_iota((1, 128)) < 64

    loads[0].wait()
    loads[1].wait()
    tile_s[...] = jnp.zeros((8, 128), F32)
    want = nb[...]
    owner = want >> 6
    peer = ((owner >> 2) - me_m + 1) * 4 + ((owner - me_x) & 3)
    opposite = lax.broadcasted_iota(jnp.int32, (6, 64), 0) ^ 1
    tile_s[0:6, 0:64] = (peer * 512 + opposite * 64 + (want & 63)).astype(F32)
    packed = tile_s[...]
    turned = pltpu.roll(packed, 64, axis=1)
    pairs = [jnp.where(low_half, packed[f:f + 1], turned[f + 1:f + 2]) for f in (0, 2, 4)]
    row = jnp.concatenate(pairs, axis=1).astype(jnp.int32)
    peer_row = row >> 9
    ident = row & 511
    hits = lax.broadcasted_iota(jnp.int32, (16, ROWS), 0) == peer_row
    rank = dot(hits.astype(F32).astype(BF16), before[...])
    base = (lax.broadcasted_iota(jnp.int32, (16, ROWS), 0) * 64).astype(F32)
    slot = jnp.sum(jnp.where(hits, rank + base, 0.0), axis=0, keepdims=True)
    slot8 = jnp.broadcast_to(slot, (8, ROWS))
    place[...] = (
        lax.broadcasted_iota(jnp.int32, (SLOTS, ROWS), 0).astype(F32) == slot
    ).astype(F32).astype(BF16)
    which = lax.broadcasted_iota(jnp.int32, (8, ROWS), 0)
    parts = jnp.where(which == 0, ident & 63, jnp.where(which == 1, ident >> 6, 0)).astype(F32).astype(BF16)
    found = lax.dot_general(parts, place[...], (((1,), (1,)), ((), ())), preferred_element_type=F32)
    codes = found[0:1] + 64.0 * found[1:2]
    for t in range(6):
        lists[t] = jnp.broadcast_to(codes[:, 128 * t:128 * t + 128], (8, 128))

    pl.semaphore_wait(barrier, PEERS - 1)
    list_sends = [remote(p, lists.at[p // 2], lists_in, list_ssem, list_rsem) for p in ORDER if p != SELF]
    for send in list_sends:
        send.start()

    slot_col = slot8.T[:, 0:1]
    place_t[...] = (lane_iota((ROWS, SLOTS)).astype(F32) == slot_col).astype(F32).astype(BF16)

    for load in loads[2:8]:
        load.wait()
    scale = jnp.left_shift(jnp.ones((1, 64), jnp.int32), level[...]).astype(F32) * 0.25
    tile_s[...] = jnp.zeros((8, 128), F32)
    tile_s[0:1, 0:64] = lam[...] * scale * scale
    tile_s[1:2, 0:64] = mu[...] * scale * scale
    tile_s[2:3, 0:64] = live[...].astype(F32)
    flat = tile_s[...].T
    for i in range(3):
        coef[i] = jnp.broadcast_to(flat[0:64, i:i + 1], (64, 128))
    tile_s[...] = jnp.zeros((8, 128), F32)
    kinds = kind[...]
    tile_s[0:6, 0:64] = jnp.where(kinds == 1, 4, jnp.where(kinds == 2, quad[...], -1)).astype(F32)
    flat = tile_s[...].T
    for f in range(6):
        code_b[64 * f:64 * f + 64] = jnp.broadcast_to(flat[0:64, f:f + 1], (64, 128))

    loads[8].wait()
    alive = jnp.concatenate([coef[2]] * 4, axis=1)
    for c in range(3):
        x[c] = x[c] * alive
    loads[9].wait()
    for i, part in enumerate(split(x[...].reshape(192, 512))):
        layers = dot(part, twice[...])
        for f in range(6):
            cut = layers[:, 128 * f:128 * f + 128]
            table[i, 64 * f:64 * f + 64, 0:128] = jnp.where(low_half, cut[0:64], cut[64:128]).astype(BF16)
            table[i, 64 * f:64 * f + 64, 128:256] = cut[128:192].astype(BF16)

    def pack(buffer, p, rows):
        buffer[p, 0:64] = rows[:, 0:128]
        buffer[p, 64:96] = jnp.where(low_half, rows[0:32, 128:256], rows[32:64, 128:256])

    def unpack(message):
        tail = message[64:96]
        other = pltpu.roll(tail, 64, axis=1)
        third = jnp.concatenate(
            [jnp.where(low_half, tail, other), jnp.where(low_half, other, tail)], axis=0
        )
        return jnp.concatenate([message[0:64], third], axis=1)

    lane_row = lane_iota((64, ROWS)).astype(F32)
    lists_in[SELF] = lists[SELF // 2]
    f_sends = []
    for group in GROUPS:
        for n, p in enumerate(group):
            if p != SELF:
                arrival(p, lists_in, list_ssem, list_rsem).wait_recv()
            column = lists_in[p].T[64 * (p % 2):64 * (p % 2) + 64, 0:1]
            sel[64 * n:64 * n + 64] = (lane_row == column).astype(F32).astype(BF16)
        chosen = sel[0:64 * len(group)]
        rows = dot(chosen, table[0]) + dot(chosen, table[1])
        for n, p in enumerate(group):
            cut = rows[64 * n:64 * n + 64]
            if p == SELF:
                pack(frecv, p, cut)
            else:
                pack(fsend, p, cut)
                send = remote(p, fsend.at[p], frecv, f_ssem, f_rsem)
                send.start()
                f_sends.append(send)

    down_iota = lax.broadcasted_iota(jnp.int32, (ROWS, 128), 0).astype(F32)
    for t in range(6):
        ids = jnp.where(low_half, lists_in[2 * t], lists_in[2 * t + 1])[0:1]
        sel_t[:, 128 * t:128 * t + 128] = (down_iota == ids).astype(F32).astype(BF16)
    loads[10].wait()

    lane = lane_iota((1, 128))
    ok_up2, ok_dn2 = (lane & 7) < 7, (lane & 7) > 0
    ok_up1, ok_dn1 = (lane & 63) < 56, (lane & 63) >= 8

    def step2(v):
        return jnp.where(ok_up2, pltpu.roll(v, 127, axis=1), 0.0) - jnp.where(ok_dn2, pltpu.roll(v, 1, axis=1), 0.0)

    def step1(v):
        return jnp.where(ok_up1, pltpu.roll(v, 120, axis=1), 0.0) - jnp.where(ok_dn1, pltpu.roll(v, 8, axis=1), 0.0)

    def step0(tiles):
        swung = [pltpu.roll(v, 64, axis=1) for v in tiles]
        none = jnp.zeros_like(swung[0])
        up = [jnp.where(low_half, swung[t], swung[t + 1] if t < 3 else none) for t in range(4)]
        dn = [jnp.where(low_half, swung[t - 1] if t > 0 else none, swung[t]) for t in range(4)]
        return [u - d for u, d in zip(up, dn)]

    pair_of = {(0, 0): 0, (1, 1): 1, (2, 2): 2, (0, 1): 3, (0, 2): 4, (1, 2): 5}

    def pair(a, b):
        return pair_of[(min(a, b), max(a, b))]

    def inner(i, _):
        rows = pl.ds(pl.multiple_of(i * 8, 8), 8)
        tiles = [[x[c, rows, 128 * t:128 * t + 128] for t in range(4)] for c in range(3)]
        first = [step0(tiles[c]) for c in range(3)]
        for t in range(4):
            cols = slice(128 * t, 128 * t + 128)
            d = [[first[c][t], step1(tiles[c][t]), step2(tiles[c][t])] for c in range(3)]
            for a in range(3):
                sym[a, rows, cols] = d[a][a]
                for b in range(a + 1, 3):
                    sym[pair(a, b), rows, cols] = d[a][b] + d[b][a]
            jac[rows, cols] = coef[1, rows] - coef[0, rows] * jnp.log(jac[rows, cols])
        return 0

    lax.fori_loop(0, 8, inner, 0)

    for load in loads[11:14]:
        load.wait()

    raw = [jnp.zeros((ROWS, 256), F32), jnp.zeros((ROWS, 256), F32)]
    for p in ORDER:
        if p != SELF:
            arrival(p, frecv, f_ssem, f_rsem).wait_recv()
    for i, part in enumerate(split(jnp.concatenate([unpack(frecv[p]) for p in range(PEERS)], axis=0))):
        raw[i] = dot(place_t[...], part)
    code = code_b[...]
    raw_b = [r.astype(BF16) for r in raw]
    ghost = []
    for part in range(2):
        cut = slice(128 * part, 128 * part + 128)
        spread = dot(raw_b[0][:, cut], fill[...]) + dot(raw_b[1][:, cut], fill[...])
        value = jnp.where(code == 4.0, raw[0][:, cut] + raw[1][:, cut], 0.0)
        for q in range(4):
            value = jnp.where(code == float(q), spread[:, 128 * q:128 * q + 128], value)
        ghost.append(value)
    for a in range(3):
        low = [-g[128 * a:128 * a + 64] for g in ghost]
        high = [g[128 * a + 64:128 * a + 128] for g in ghost]
        sides = jnp.concatenate(
            [
                jnp.where(low_half, low[0], pltpu.roll(high[0], 64, axis=1)),
                jnp.where(low_half, pltpu.roll(low[0], 64, axis=1), high[0]),
                jnp.where(low_half, low[1], high[1]),
            ],
            axis=0,
        )
        h, l = split(sides)
        weights = inject[128 * a:128 * a + 128]
        inj[a] = (dot(h, weights) + dot(l, weights)).reshape(3, 64, 512)

    def stress(i, _):
        rows = pl.ds(pl.multiple_of(i * 8, 8), 8)
        for t in range(4):
            cols = slice(128 * t, 128 * t + 128)
            shear = jac[rows, cols]
            diag = [sym[a, rows, cols] + inj[a, a, rows, cols] for a in range(3)]
            trace = coef[0, rows] * (diag[0] + diag[1] + diag[2])
            for a in range(3):
                sym[a, rows, cols] = trace + 2.0 * shear * diag[a]
                for b in range(a + 1, 3):
                    both = sym[pair(a, b), rows, cols] + inj[a, b, rows, cols] + inj[b, a, rows, cols]
                    sym[pair(a, b), rows, cols] = shear * both
        return 0

    lax.fori_loop(0, 8, stress, 0)

    bars = [[None] * 6 for _ in range(2)]
    for a in range(3):
        stacked = jnp.concatenate([sym[pair(c, a)] for c in range(3)], axis=0)
        for i, part in enumerate(split(stacked)):
            layers = dot(part, twice[:, 256 * a:256 * a + 256])
            for side in range(2):
                cut = layers[:, 128 * side:128 * side + 128]
                if side == 0:
                    cut = -cut
                bars[i][2 * a + side] = jnp.concatenate(
                    [jnp.where(low_half, cut[0:64], cut[64:128]), cut[128:192]], axis=1
                )
    bar = [jnp.concatenate(b, axis=0) for b in bars]
    bar_b = [b.astype(BF16) for b in bar]
    leaving = []
    for part in range(2):
        cut = slice(128 * part, 128 * part + 128)
        spread = dot(bar_b[0][:, cut], unfill[...]) + dot(bar_b[1][:, cut], unfill[...])
        value = jnp.where(code == 4.0, bar[0][:, cut] + bar[1][:, cut], 0.0)
        for q in range(4):
            value = jnp.where(code == float(q), spread[:, 128 * q:128 * q + 128], value)
        leaving.append(value)
    h, l = split(jnp.concatenate(leaving, axis=1))
    a_sends = []
    for group in GROUPS:
        for p in group:
            chosen = place[64 * p:64 * p + 64]
            cut = dot(chosen, h) + dot(chosen, l)
            if p == SELF:
                pack(arecv, p, cut)
            else:
                pack(asend, p, cut)
                send = remote(p, asend.at[p], arecv, a_ssem, a_rsem)
                send.start()
                a_sends.append(send)

    def outer(i, _):
        rows = pl.ds(pl.multiple_of(i * 8, 8), 8)
        for c in range(3):
            first = step0([sym[pair(c, 0), rows, 128 * t:128 * t + 128] for t in range(4)])
            for t in range(4):
                cols = slice(128 * t, 128 * t + 128)
                back[c, rows, cols] = -(
                    first[t] + step1(sym[pair(c, 1), rows, cols]) + step2(sym[pair(c, 2), rows, cols])
                )
        return 0

    lax.fori_loop(0, 8, outer, 0)

    for p in ORDER:
        if p != SELF:
            arrival(p, arecv, a_ssem, a_rsem).wait_recv()
    h, l = split(jnp.concatenate([unpack(arecv[p]) for p in range(PEERS)], axis=0))
    landed_rows[...] = dot(sel_t[...], h) + dot(sel_t[...], l)
    total = jnp.zeros((192, 512), F32)
    for a in range(3):
        low = landed_rows[128 * a:128 * a + 64]
        high = landed_rows[128 * a + 64:128 * a + 128]
        sides = jnp.concatenate(
            [
                jnp.where(low_half, low[:, 0:128], pltpu.roll(high[:, 0:128], 64, axis=1)),
                jnp.where(low_half, pltpu.roll(low[:, 0:128], 64, axis=1), high[:, 0:128]),
                jnp.where(low_half, low[:, 128:256], high[:, 128:256]),
            ],
            axis=0,
        )
        h, l = split(sides)
        weights = inject[128 * a:128 * a + 128]
        total = total + dot(h, weights) + dot(l, weights)
    for c in range(3):
        out_ref[c] = (back[c] + total[64 * c:64 * c + 64]) * alive

    for send in list_sends + f_sends + a_sends:
        send.wait_send()


def per_device(
    direction, jacobian, shear_modulus, lame_modulus, refine_level, live_flag, neighbor, face_kind, face_quadrant
):
    ranges = lax.axis_size("morton")
    consts = tables()
    operands = [
        jnp.transpose(direction, (1, 0, 2)),
        jacobian,
        shear_modulus[None, :],
        lame_modulus[None, :],
        refine_level[None, :],
        live_flag[None, :],
        neighbor.T,
        face_kind.T,
        face_quadrant.T,
    ] + consts
    buffers = [pltpu.VMEM(o.shape, o.dtype) for o in operands]
    message = pltpu.VMEM((PEERS, 96, 128), F32)
    peers = pltpu.SemaphoreType.DMA((PEERS,))
    result = pl.pallas_call(
        functools.partial(kernel, ranges),
        out_shape=jax.ShapeDtypeStruct((3, BLOCKS, 512), F32),
        in_specs=[pl.BlockSpec(memory_space=pl.ANY)] * len(operands),
        out_specs=pl.BlockSpec(memory_space=pltpu.VMEM),
        scratch_shapes=buffers
        + [
            pltpu.VMEM((8, 128), F32),
            pltpu.VMEM((ROWS, 128), F32),
            pltpu.VMEM((3, 64, 128), F32),
            pltpu.VMEM((2, ROWS, 256), BF16),
            pltpu.VMEM((ROWS, ROWS), BF16),
            pltpu.VMEM((ROWS, SLOTS), BF16),
            pltpu.VMEM((SLOTS, ROWS), BF16),
            pltpu.VMEM((ROWS, SLOTS), BF16),
            pltpu.VMEM((6, 8, 128), F32),
            pltpu.VMEM((PEERS, 8, 128), F32),
            message,
            message,
            message,
            message,
            pltpu.VMEM((ROWS, 256), F32),
            pltpu.VMEM((6, 64, 512), F32),
            pltpu.VMEM((3, 3, 64, 512), F32),
            pltpu.VMEM((3, 64, 512), F32),
            pltpu.SemaphoreType.DMA((len(operands),)),
            peers,
            peers,
            peers,
            peers,
            peers,
            peers,
        ],
        compiler_params=pltpu.CompilerParams(
            collective_id=0, has_side_effects=True, vmem_limit_bytes=40 * 1024 * 1024
        ),
        name="hessian_exchange",
    )(*operands)
    return jnp.transpose(result, (1, 0, 2))


def solution(mesh):
    in_specs = (
        P(("morton", "sub"), None, None),
        P(("morton", "sub"), None),
        P(("morton", "sub")),
        P(("morton", "sub")),
        P(("morton", "sub")),
        P(("morton", "sub")),
        P(("morton", "sub"), None),
        P(("morton", "sub"), None),
        P(("morton", "sub"), None),
    )
    out_specs = P(("morton", "sub"), None, None)
    return jax.shard_map(
        per_device, mesh=mesh, in_specs=in_specs, out_specs=out_specs, check_vma=False
    )
```

```python
import functools

import jax
import jax.numpy as jnp
import numpy as np
from jax import lax
from jax.experimental import pallas as pl
from jax.experimental.pallas import tpu as pltpu
from jax.sharding import PartitionSpec as P

BLOCKS = 64
ROWS = 6 * BLOCKS
PEERS = 12
SLOTS = PEERS * BLOCKS
SELF = 4
F32 = jnp.float32
BF16 = jnp.bfloat16
MESH = pl.DeviceIdType.MESH
GROUPS = ((2, 6, 10), (1, 3, 5, 7, 9, 11), (0, 8, 4))
ORDER = tuple(p for group in GROUPS for p in group)
OTHERS = tuple(p for p in ORDER if p != SELF)


def tables():
    node = np.arange(512)
    coords = (node // 64, (node // 8) % 8, node % 8)
    pick = np.zeros((512, 6, 64), np.float32)
    for face in range(6):
        axis = face // 2
        others = [coords[a] for a in range(3) if a != axis]
        for n in np.nonzero(coords[axis] == 7 * (face % 2))[0]:
            pick[n, face, others[0][n] * 8 + others[1][n]] = 1
    halves = np.zeros((2, 8, 8), np.float32)
    for u in range(2):
        for i in range(8):
            halves[u, i, (7 * u + i) // 2] += 0.5
            halves[u, i, (7 * u + i + 1) // 2] += 0.5
    fill = np.zeros((128, 512), np.float32)
    unfill = np.zeros((128, 512), np.float32)
    for q in range(4):
        spread = np.kron(halves[q // 2], halves[q % 2])
        for half in range(2):
            lanes = slice(64 * half, 64 * half + 64)
            cols = slice(128 * q + 64 * half, 128 * q + 64 * half + 64)
            fill[lanes, cols] = spread.T
            unfill[lanes, cols] = spread
    twice = np.concatenate([pick, pick], axis=2).reshape(512, 768)
    inject = pick.reshape(512, ROWS).T
    before = np.triu(np.ones((ROWS, ROWS), np.float32), 1)
    return [jnp.asarray(t, BF16) for t in (twice, inject, fill, unfill, before)]


def split(values):
    high = values.astype(BF16)
    low = (values - high.astype(F32)).astype(BF16)
    return high, low


def dot(a, b):
    return jnp.dot(a, b, preferred_element_type=F32)


def lane_iota(shape):
    return lax.broadcasted_iota(jnp.int32, shape, len(shape) - 1)


def kernel(
    ranges,
    x_hbm, jac_hbm, mu_hbm, lam_hbm, level_hbm, live_hbm, nb_hbm, kind_hbm, quad_hbm,
    twice_hbm, inject_hbm, fill_hbm, unfill_hbm, before_hbm,
    out_ref,
    x, jac, mu, lam, level, live, nb, kind, quad,
    twice, inject, fill, unfill, before,
    tile_s, code_b, coef, table, sel, sel_t, place, place_t, lists, lists_in,
    fsend, frecv, asend, arecv, landed_rows, sym, inj, back,
    in_sem, list_ssem, list_rsem, f_ssem, f_rsem, a_ssem, a_rsem,
):
    me_m = lax.axis_index("morton")
    me_x = lax.axis_index("sub")

    has_low = me_m > 0
    has_high = me_m < ranges - 1
    present = 3 + 4 * has_low.astype(jnp.int32) + 4 * has_high.astype(jnp.int32)

    def device(p):
        return (me_m + (p // 4 - 1), lax.rem(me_x + p % 4, 4))

    def guarded(p, act):
        if p // 4 == 1:
            act()
        else:
            pl.when(has_low if p // 4 == 0 else has_high)(act)


    def mirror(p):
        return (2 - p // 4) * 4 + (4 - p % 4) % 4

    def remote(p, src, dst, ssem, rsem):
        return pltpu.make_async_remote_copy(
            src_ref=src, dst_ref=dst.at[mirror(p)], send_sem=ssem.at[p], recv_sem=rsem.at[mirror(p)],
            device_id=device(p), device_id_type=MESH,
        )

    def arrival(p, dst, ssem, rsem):
        return pltpu.make_async_remote_copy(
            src_ref=dst.at[p], dst_ref=dst.at[p], send_sem=ssem.at[p], recv_sem=rsem.at[p],
            device_id=device(p), device_id_type=MESH,
        )

    loads = [
        pltpu.make_async_copy(src, dst, in_sem.at[i])
        for i, (src, dst) in enumerate(
            (
                (nb_hbm, nb), (before_hbm, before), (kind_hbm, kind), (quad_hbm, quad),
                (live_hbm, live), (mu_hbm, mu), (lam_hbm, lam), (level_hbm, level),
                (x_hbm, x), (twice_hbm, twice), (jac_hbm, jac), (inject_hbm, inject),
                (fill_hbm, fill), (unfill_hbm, unfill),
            )
        )
    ]
    for load in loads:
        load.start()
    barrier = pltpu.get_barrier_semaphore()
    for p in OTHERS:
        guarded(p, lambda p=p: pl.semaphore_signal(barrier, inc=1, device_id=device(p), device_id_type=MESH))

    low_half = lane_iota((1, 128)) < 64

    def clear(first):
        for buffer in (frecv, arecv):
            buffer[first:first + 4] = jnp.zeros((4, 96, 128), F32)
        lists_in[first:first + 4] = jnp.zeros((4, 8, 128), F32)

    pl.when(jnp.logical_not(has_low))(lambda: clear(0))
    pl.when(jnp.logical_not(has_high))(lambda: clear(8))

    loads[0].wait()
    loads[1].wait()
    tile_s[...] = jnp.zeros((8, 128), F32)
    want = nb[...]
    owner = want >> 6
    peer = ((owner >> 2) - me_m + 1) * 4 + ((owner - me_x) & 3)
    opposite = lax.broadcasted_iota(jnp.int32, (6, 64), 0) ^ 1
    tile_s[0:6, 0:64] = (peer * 512 + opposite * 64 + (want & 63)).astype(F32)
    packed = tile_s[...]
    turned = pltpu.roll(packed, 64, axis=1)
    pairs = [jnp.where(low_half, packed[f:f + 1], turned[f + 1:f + 2]) for f in (0, 2, 4)]
    row = jnp.concatenate(pairs, axis=1).astype(jnp.int32)
    peer_row = row >> 9
    ident = row & 511
    hits = lax.broadcasted_iota(jnp.int32, (16, ROWS), 0) == peer_row
    rank = dot(hits.astype(F32).astype(BF16), before[...])
    base = (lax.broadcasted_iota(jnp.int32, (16, ROWS), 0) * 64).astype(F32)
    slot = jnp.sum(jnp.where(hits, rank + base, 0.0), axis=0, keepdims=True)
    slot8 = jnp.broadcast_to(slot, (8, ROWS))
    place[...] = (
        lax.broadcasted_iota(jnp.int32, (SLOTS, ROWS), 0).astype(F32) == slot
    ).astype(F32).astype(BF16)
    which = lax.broadcasted_iota(jnp.int32, (8, ROWS), 0)
    parts = jnp.where(which == 0, ident & 63, jnp.where(which == 1, ident >> 6, 0)).astype(F32).astype(BF16)
    found = lax.dot_general(parts, place[...], (((1,), (1,)), ((), ())), preferred_element_type=F32)
    codes = found[0:1] + 64.0 * found[1:2]
    for t in range(6):
        lists[t] = jnp.broadcast_to(codes[:, 128 * t:128 * t + 128], (8, 128))

    pl.semaphore_wait(barrier, present)
    sends = []

    def start(send, p):
        guarded(p, send.start)
        sends.append((p, send))

    def await_rows(p, dst, ssem, rsem):
        guarded(p, arrival(p, dst, ssem, rsem).wait_recv)

    for p in OTHERS:
        start(remote(p, lists.at[p // 2], lists_in, list_ssem, list_rsem), p)

    slot_col = slot8.T[:, 0:1]
    place_t[...] = (lane_iota((ROWS, SLOTS)).astype(F32) == slot_col).astype(F32).astype(BF16)

    for load in loads[2:8]:
        load.wait()
    scale = jnp.left_shift(jnp.ones((1, 64), jnp.int32), level[...]).astype(F32) * 0.25
    tile_s[...] = jnp.zeros((8, 128), F32)
    tile_s[0:1, 0:64] = lam[...] * scale * scale
    tile_s[1:2, 0:64] = mu[...] * scale * scale
    tile_s[2:3, 0:64] = live[...].astype(F32)
    flat = tile_s[...].T
    for i in range(3):
        coef[i] = jnp.broadcast_to(flat[0:64, i:i + 1], (64, 128))
    tile_s[...] = jnp.zeros((8, 128), F32)
    kinds = kind[...]
    tile_s[0:6, 0:64] = jnp.where(kinds == 1, 4, jnp.where(kinds == 2, quad[...], -1)).astype(F32)
    flat = tile_s[...].T
    for f in range(6):
        code_b[64 * f:64 * f + 64] = jnp.broadcast_to(flat[0:64, f:f + 1], (64, 128))

    loads[8].wait()
    alive = jnp.concatenate([coef[2]] * 4, axis=1)
    for c in range(3):
        x[c] = x[c] * alive
    loads[9].wait()
    for i, part in enumerate(split(x[...].reshape(192, 512))):
        layers = dot(part, twice[...])
        for f in range(6):
            cut = layers[:, 128 * f:128 * f + 128]
            table[i, 64 * f:64 * f + 64, 0:128] = jnp.where(low_half, cut[0:64], cut[64:128]).astype(BF16)
            table[i, 64 * f:64 * f + 64, 128:256] = cut[128:192].astype(BF16)

    def pack(buffer, p, rows):
        buffer[p, 0:64] = rows[:, 0:128]
        buffer[p, 64:96] = jnp.where(low_half, rows[0:32, 128:256], rows[32:64, 128:256])

    def unpack(message):
        tail = message[64:96]
        other = pltpu.roll(tail, 64, axis=1)
        third = jnp.concatenate(
            [jnp.where(low_half, tail, other), jnp.where(low_half, other, tail)], axis=0
        )
        return jnp.concatenate([message[0:64], third], axis=1)

    lane_row = lane_iota((64, ROWS)).astype(F32)
    lists_in[SELF] = lists[SELF // 2]
    for group in GROUPS:
        for n, p in enumerate(group):
            if p != SELF:
                await_rows(p, lists_in, list_ssem, list_rsem)
            column = lists_in[p].T[64 * (p % 2):64 * (p % 2) + 64, 0:1]
            sel[64 * n:64 * n + 64] = (lane_row == column).astype(F32).astype(BF16)
        chosen = sel[0:64 * len(group)]
        rows = dot(chosen, table[0]) + dot(chosen, table[1])
        for n, p in enumerate(group):
            cut = rows[64 * n:64 * n + 64]
            if p == SELF:
                pack(frecv, p, cut)
            else:
                pack(fsend, p, cut)
                start(remote(p, fsend.at[p], frecv, f_ssem, f_rsem), p)

    down_iota = lax.broadcasted_iota(jnp.int32, (ROWS, 128), 0).astype(F32)
    for t in range(6):
        ids = jnp.where(low_half, lists_in[2 * t], lists_in[2 * t + 1])[0:1]
        sel_t[:, 128 * t:128 * t + 128] = (down_iota == ids).astype(F32).astype(BF16)
    loads[10].wait()

    lane = lane_iota((1, 128))
    ok_up2, ok_dn2 = (lane & 7) < 7, (lane & 7) > 0
    ok_up1, ok_dn1 = (lane & 63) < 56, (lane & 63) >= 8

    def step2(v):
        return jnp.where(ok_up2, pltpu.roll(v, 127, axis=1), 0.0) - jnp.where(ok_dn2, pltpu.roll(v, 1, axis=1), 0.0)

    def step1(v):
        return jnp.where(ok_up1, pltpu.roll(v, 120, axis=1), 0.0) - jnp.where(ok_dn1, pltpu.roll(v, 8, axis=1), 0.0)

    def step0(tiles):
        swung = [pltpu.roll(v, 64, axis=1) for v in tiles]
        none = jnp.zeros_like(swung[0])
        up = [jnp.where(low_half, swung[t], swung[t + 1] if t < 3 else none) for t in range(4)]
        dn = [jnp.where(low_half, swung[t - 1] if t > 0 else none, swung[t]) for t in range(4)]
        return [u - d for u, d in zip(up, dn)]

    pair_of = {(0, 0): 0, (1, 1): 1, (2, 2): 2, (0, 1): 3, (0, 2): 4, (1, 2): 5}

    def pair(a, b):
        return pair_of[(min(a, b), max(a, b))]

    def inner(i, _):
        rows = pl.ds(pl.multiple_of(i * 8, 8), 8)
        tiles = [[x[c, rows, 128 * t:128 * t + 128] for t in range(4)] for c in range(3)]
        first = [step0(tiles[c]) for c in range(3)]
        for t in range(4):
            cols = slice(128 * t, 128 * t + 128)
            d = [[first[c][t], step1(tiles[c][t]), step2(tiles[c][t])] for c in range(3)]
            for a in range(3):
                sym[a, rows, cols] = d[a][a]
                for b in range(a + 1, 3):
                    sym[pair(a, b), rows, cols] = d[a][b] + d[b][a]
            jac[rows, cols] = coef[1, rows] - coef[0, rows] * jnp.log(jac[rows, cols])
        return 0

    lax.fori_loop(0, 8, inner, 0)

    for load in loads[11:14]:
        load.wait()

    raw = [jnp.zeros((ROWS, 256), F32), jnp.zeros((ROWS, 256), F32)]
    for p in OTHERS:
        await_rows(p, frecv, f_ssem, f_rsem)
    for i, part in enumerate(split(jnp.concatenate([unpack(frecv[p]) for p in range(PEERS)], axis=0))):
        raw[i] = dot(place_t[...], part)
    code = code_b[...]
    raw_b = [r.astype(BF16) for r in raw]
    ghost = []
    for part in range(2):
        cut = slice(128 * part, 128 * part + 128)
        spread = dot(raw_b[0][:, cut], fill[...]) + dot(raw_b[1][:, cut], fill[...])
        value = jnp.where(code == 4.0, raw[0][:, cut] + raw[1][:, cut], 0.0)
        for q in range(4):
            value = jnp.where(code == float(q), spread[:, 128 * q:128 * q + 128], value)
        ghost.append(value)
    for a in range(3):
        low = [-g[128 * a:128 * a + 64] for g in ghost]
        high = [g[128 * a + 64:128 * a + 128] for g in ghost]
        sides = jnp.concatenate(
            [
                jnp.where(low_half, low[0], pltpu.roll(high[0], 64, axis=1)),
                jnp.where(low_half, pltpu.roll(low[0], 64, axis=1), high[0]),
                jnp.where(low_half, low[1], high[1]),
            ],
            axis=0,
        )
        h, l = split(sides)
        weights = inject[128 * a:128 * a + 128]
        inj[a] = (dot(h, weights) + dot(l, weights)).reshape(3, 64, 512)

    def stress(i, _):
        rows = pl.ds(pl.multiple_of(i * 8, 8), 8)
        for t in range(4):
            cols = slice(128 * t, 128 * t + 128)
            shear = jac[rows, cols]
            diag = [sym[a, rows, cols] + inj[a, a, rows, cols] for a in range(3)]
            trace = coef[0, rows] * (diag[0] + diag[1] + diag[2])
            for a in range(3):
                sym[a, rows, cols] = trace + 2.0 * shear * diag[a]
                for b in range(a + 1, 3):
                    both = sym[pair(a, b), rows, cols] + inj[a, b, rows, cols] + inj[b, a, rows, cols]
                    sym[pair(a, b), rows, cols] = shear * both
        return 0

    lax.fori_loop(0, 8, stress, 0)

    bars = [[None] * 6 for _ in range(2)]
    for a in range(3):
        stacked = jnp.concatenate([sym[pair(c, a)] for c in range(3)], axis=0)
        for i, part in enumerate(split(stacked)):
            layers = dot(part, twice[:, 256 * a:256 * a + 256])
            for side in range(2):
                cut = layers[:, 128 * side:128 * side + 128]
                if side == 0:
                    cut = -cut
                bars[i][2 * a + side] = jnp.concatenate(
                    [jnp.where(low_half, cut[0:64], cut[64:128]), cut[128:192]], axis=1
                )
    bar = [jnp.concatenate(b, axis=0) for b in bars]
    bar_b = [b.astype(BF16) for b in bar]
    leaving = []
    for part in range(2):
        cut = slice(128 * part, 128 * part + 128)
        spread = dot(bar_b[0][:, cut], unfill[...]) + dot(bar_b[1][:, cut], unfill[...])
        value = jnp.where(code == 4.0, bar[0][:, cut] + bar[1][:, cut], 0.0)
        for q in range(4):
            value = jnp.where(code == float(q), spread[:, 128 * q:128 * q + 128], value)
        leaving.append(value)
    h, l = split(jnp.concatenate(leaving, axis=1))
    for group in GROUPS:
        for p in group:
            chosen = place[64 * p:64 * p + 64]
            cut = dot(chosen, h) + dot(chosen, l)
            if p == SELF:
                pack(arecv, p, cut)
            else:
                pack(asend, p, cut)
                start(remote(p, asend.at[p], arecv, a_ssem, a_rsem), p)

    def outer(i, _):
        rows = pl.ds(pl.multiple_of(i * 8, 8), 8)
        for c in range(3):
            first = step0([sym[pair(c, 0), rows, 128 * t:128 * t + 128] for t in range(4)])
            for t in range(4):
                cols = slice(128 * t, 128 * t + 128)
                back[c, rows, cols] = -(
                    first[t] + step1(sym[pair(c, 1), rows, cols]) + step2(sym[pair(c, 2), rows, cols])
                )
        return 0

    lax.fori_loop(0, 8, outer, 0)

    for p in OTHERS:
        await_rows(p, arecv, a_ssem, a_rsem)
    h, l = split(jnp.concatenate([unpack(arecv[p]) for p in range(PEERS)], axis=0))
    landed_rows[...] = dot(sel_t[...], h) + dot(sel_t[...], l)
    total = jnp.zeros((192, 512), F32)
    for a in range(3):
        low = landed_rows[128 * a:128 * a + 64]
        high = landed_rows[128 * a + 64:128 * a + 128]
        sides = jnp.concatenate(
            [
                jnp.where(low_half, low[:, 0:128], pltpu.roll(high[:, 0:128], 64, axis=1)),
                jnp.where(low_half, pltpu.roll(low[:, 0:128], 64, axis=1), high[:, 0:128]),
                jnp.where(low_half, low[:, 128:256], high[:, 128:256]),
            ],
            axis=0,
        )
        h, l = split(sides)
        weights = inject[128 * a:128 * a + 128]
        total = total + dot(h, weights) + dot(l, weights)
    for c in range(3):
        out_ref[c] = (back[c] + total[64 * c:64 * c + 64]) * alive

    for p, send in sends:
        guarded(p, send.wait_send)


def per_device(
    direction, jacobian, shear_modulus, lame_modulus, refine_level, live_flag, neighbor, face_kind, face_quadrant
):
    ranges = lax.axis_size("morton")
    consts = tables()
    operands = [
        jnp.transpose(direction, (1, 0, 2)),
        jacobian,
        shear_modulus[None, :],
        lame_modulus[None, :],
        refine_level[None, :],
        live_flag[None, :],
        neighbor.T,
        face_kind.T,
        face_quadrant.T,
    ] + consts
    buffers = [pltpu.VMEM(o.shape, o.dtype) for o in operands]
    operands = [pltpu.with_memory_space_constraint(o, pltpu.HBM) for o in operands]
    message = pltpu.VMEM((PEERS, 96, 128), F32)
    peers = pltpu.SemaphoreType.DMA((PEERS,))
    result = pl.pallas_call(
        functools.partial(kernel, ranges),
        out_shape=jax.ShapeDtypeStruct((3, BLOCKS, 512), F32),
        in_specs=[pl.BlockSpec(memory_space=pltpu.HBM)] * len(operands),
        out_specs=pl.BlockSpec(memory_space=pltpu.VMEM),
        scratch_shapes=buffers
        + [
            pltpu.VMEM((8, 128), F32),
            pltpu.VMEM((ROWS, 128), F32),
            pltpu.VMEM((3, 64, 128), F32),
            pltpu.VMEM((2, ROWS, 256), BF16),
            pltpu.VMEM((ROWS, ROWS), BF16),
            pltpu.VMEM((ROWS, SLOTS), BF16),
            pltpu.VMEM((SLOTS, ROWS), BF16),
            pltpu.VMEM((ROWS, SLOTS), BF16),
            pltpu.VMEM((6, 8, 128), F32),
            pltpu.VMEM((PEERS, 8, 128), F32),
            message,
            message,
            message,
            message,
            pltpu.VMEM((ROWS, 256), F32),
            pltpu.VMEM((6, 64, 512), F32),
            pltpu.VMEM((3, 3, 64, 512), F32),
            pltpu.VMEM((3, 64, 512), F32),
            pltpu.SemaphoreType.DMA((len(operands),)),
            peers,
            peers,
            peers,
            peers,
            peers,
            peers,
        ],
        compiler_params=pltpu.CompilerParams(
            collective_id=0, has_side_effects=True, vmem_limit_bytes=48 * 1024 * 1024
        ),
        name="hessian_exchange",
    )(*operands)
    return jnp.transpose(result, (1, 0, 2))


def solution(mesh):
    in_specs = (
        P(("morton", "sub"), None, None),
        P(("morton", "sub"), None),
        P(("morton", "sub")),
        P(("morton", "sub")),
        P(("morton", "sub")),
        P(("morton", "sub")),
        P(("morton", "sub"), None),
        P(("morton", "sub"), None),
        P(("morton", "sub"), None),
    )
    out_specs = P(("morton", "sub"), None, None)
    return jax.shard_map(
        per_device, mesh=mesh, in_specs=in_specs, out_specs=out_specs, check_vma=False
    )
```

```python
import functools

import jax
import jax.numpy as jnp
import numpy as np
from jax import lax
from jax.experimental import pallas as pl
from jax.experimental.pallas import tpu as pltpu
from jax.sharding import PartitionSpec as P

BLOCKS = 64
ROWS = 6 * BLOCKS
PEERS = 12
SLOTS = PEERS * BLOCKS
F32 = jnp.float32
BF16 = jnp.bfloat16
MESH = pl.DeviceIdType.MESH
STEPS = (1, 3, 2, 0)
SELF = 10
OTHERS = (6, 8, 7, 0, 2, 3, 5, 1, 4, 9, 11)
ARRIVALS = (3, 2, 0, 1)
PAIRS = {(0, 0): 0, (1, 1): 1, (2, 2): 2, (0, 1): 3, (0, 2): 4, (1, 2): 5}


def pair(a, b):
    return PAIRS[(min(a, b), max(a, b))]


def mirror(q):
    return 3 * STEPS.index((4 - STEPS[q // 3]) % 4) + 2 - q % 3


def tables():
    node = np.arange(512)
    coords = (node // 64, (node // 8) % 8, node % 8)
    pick = np.zeros((512, 6, 64), np.float32)
    for face in range(6):
        axis = face // 2
        others = [coords[a] for a in range(3) if a != axis]
        for n in np.nonzero(coords[axis] == 7 * (face % 2))[0]:
            pick[n, face, others[0][n] * 8 + others[1][n]] = 1
    halves = np.zeros((2, 8, 8), np.float32)
    for u in range(2):
        for i in range(8):
            halves[u, i, (7 * u + i) // 2] += 0.5
            halves[u, i, (7 * u + i + 1) // 2] += 0.5
    fill = np.zeros((128, 512), np.float32)
    unfill = np.zeros((128, 512), np.float32)
    for q in range(4):
        spread = np.kron(halves[q // 2], halves[q % 2])
        for half in range(2):
            lanes = slice(64 * half, 64 * half + 64)
            cols = slice(128 * q + 64 * half, 128 * q + 64 * half + 64)
            fill[lanes, cols] = spread.T
            unfill[lanes, cols] = spread
    twice = np.concatenate([pick, pick], axis=2).reshape(512, 768)
    inject = pick.reshape(512, 3, 128).transpose(1, 2, 0)
    inject = np.concatenate([inject, inject], axis=1).reshape(768, 512)
    before = np.triu(np.ones((ROWS, ROWS), np.float32), 1)
    stacked = (np.concatenate([t, t], axis=0) for t in (fill, unfill))
    return [jnp.asarray(t, BF16) for t in (twice, inject, *stacked, before)]


def split(values, axis):
    high = values.astype(BF16)
    low = (values - high.astype(F32)).astype(BF16)
    return jnp.concatenate([high, low], axis=axis)


def dot(a, b):
    return jnp.dot(a, b, preferred_element_type=F32)


def lane_iota(shape):
    return lax.broadcasted_iota(jnp.int32, shape, len(shape) - 1)


def row_iota(shape):
    return lax.broadcasted_iota(jnp.int32, shape, 0)


def one_hot(hits):
    return hits.astype(F32).astype(BF16)


def kernel(
    ranges,
    x_hbm, jac_hbm, mu_hbm, lam_hbm, level_hbm, live_hbm, nb_hbm, kind_hbm, quad_hbm,
    twice_hbm, inject_hbm, fill_hbm, unfill_hbm, before_hbm,
    out_ref,
    x, jac, mu, lam, level, live, nb, kind, quad,
    twice, inject, fill, unfill, before,
    tile_s, code_b, coef, table, sel_t, place, place_t, lists, lists_in,
    fsend, frecv, asend, arecv, gathered, leaving, sym, inj, back,
    in_sem, list_ssem, list_rsem, f_ssem, f_rsem, a_ssem, a_rsem,
):
    me_m = lax.axis_index("morton")
    me_x = lax.axis_index("sub")
    has_low = me_m > 0
    has_high = me_m < ranges - 1
    present = 3 + 4 * has_low.astype(jnp.int32) + 4 * has_high.astype(jnp.int32)
    low_half = lane_iota((1, 128)) < 64

    def device(q):
        return (me_m + (q % 3 - 1), lax.rem(me_x + STEPS[q // 3], 4))

    def guarded(q, act):
        if q % 3 == 1:
            act()
        else:
            pl.when(has_low if q % 3 == 0 else has_high)(act)

    sends = []

    def send(q, src, dst, ssem, rsem):
        copy = pltpu.make_async_remote_copy(
            src_ref=src.at[q], dst_ref=dst.at[mirror(q)], send_sem=ssem.at[q], recv_sem=rsem.at[mirror(q)],
            device_id=device(q), device_id_type=MESH,
        )
        guarded(q, copy.start)
        sends.append((q, copy))

    def arrive(q, dst, ssem, rsem):
        copy = pltpu.make_async_remote_copy(
            src_ref=dst.at[q], dst_ref=dst.at[q], send_sem=ssem.at[q], recv_sem=rsem.at[q],
            device_id=device(q), device_id_type=MESH,
        )
        guarded(q, copy.wait_recv)

    loads = [
        pltpu.make_async_copy(src, dst, in_sem.at[i])
        for i, (src, dst) in enumerate(
            (
                (nb_hbm, nb), (before_hbm, before), (kind_hbm, kind), (quad_hbm, quad),
                (live_hbm, live), (mu_hbm, mu), (lam_hbm, lam), (level_hbm, level),
                (x_hbm, x), (twice_hbm, twice), (jac_hbm, jac), (inject_hbm, inject),
                (fill_hbm, fill), (unfill_hbm, unfill),
            )
        )
    ]

    def loaded(first, last):
        for load in loads[first:last]:
            load.wait()

    def clear(first):
        for q in range(first, PEERS, 3):
            frecv[q] = jnp.zeros((96, 128), F32)
            arecv[q] = jnp.zeros((96, 128), F32)
            lists_in[q] = jnp.zeros((8, 128), F32)

    def request():
        loaded(0, 2)
        tile_s[...] = jnp.zeros((8, 128), F32)
        want = nb[...]
        owner = want >> 6
        step = (owner - me_x) & 3
        group = jnp.where(step == 1, 0, jnp.where(step == 3, 1, jnp.where(step == 2, 2, 3)))
        peer = group * 3 + ((owner >> 2) - me_m + 1)
        opposite = row_iota((6, 64)) ^ 1
        tile_s[0:6, 0:64] = (peer * 512 + opposite * 64 + (want & 63)).astype(F32)
        packed = tile_s[...]
        turned = pltpu.roll(packed, 64, axis=1)
        pairs = [jnp.where(low_half, packed[f:f + 1], turned[f + 1:f + 2]) for f in (0, 2, 4)]
        row = jnp.concatenate(pairs, axis=1).astype(jnp.int32)
        ident = row & 511
        hits = row_iota((16, ROWS)) == (row >> 9)
        rank = dot(one_hot(hits), before[...])
        base = (row_iota((16, ROWS)) * 64).astype(F32)
        slot = jnp.sum(jnp.where(hits, rank + base, 0.0), axis=0, keepdims=True)
        place[...] = one_hot(row_iota((SLOTS, ROWS)).astype(F32) == slot)
        which = row_iota((8, ROWS))
        parts = jnp.where(which == 0, ident & 63, jnp.where(which == 1, ident >> 6, 0))
        found = lax.dot_general(
            parts.astype(F32).astype(BF16), place[...], (((1,), (1,)), ((), ())), preferred_element_type=F32
        )
        codes = jnp.broadcast_to(found[0:1] + 64.0 * found[1:2], (8, SLOTS))
        for t in range(PEERS // 2):
            both = codes[:, 128 * t:128 * t + 128]
            swapped = pltpu.roll(both, 64, axis=1)
            lists[2 * t] = jnp.where(low_half, both, swapped)
            lists[2 * t + 1] = jnp.where(low_half, swapped, both)
        return slot

    def prepare(slot):
        slot_col = jnp.broadcast_to(slot, (8, ROWS)).T[:, 0:1]
        lanes = lane_iota((ROWS, ROWS))
        lanes = jnp.where(lanes < 192, lanes, lanes - 192).astype(F32)
        for i in range(4):
            place_t[i] = one_hot(lanes == slot_col - 192.0 * i)
        loaded(2, 8)
        scale = jnp.left_shift(jnp.ones((1, 64), jnp.int32), level[...]).astype(F32) * 0.25
        tile_s[...] = jnp.zeros((8, 128), F32)
        tile_s[0:1, 0:64] = lam[...] * scale * scale
        tile_s[1:2, 0:64] = mu[...] * scale * scale
        tile_s[2:3, 0:64] = live[...].astype(F32)
        flat = tile_s[...].T
        for i in range(3):
            coef[i] = jnp.broadcast_to(flat[0:64, i:i + 1], (64, 128))
        tile_s[...] = jnp.zeros((8, 128), F32)
        kinds = kind[...]
        tile_s[0:6, 0:64] = jnp.where(kinds == 1, 4, jnp.where(kinds == 2, quad[...], -1)).astype(F32)
        flat = tile_s[...].T
        for f in range(6):
            code_b[64 * f:64 * f + 64] = jnp.broadcast_to(flat[0:64, f:f + 1], (64, 128))
        loaded(8, 9)
        alive = jnp.concatenate([coef[2]] * 4, axis=1)
        for c in range(3):
            x[c] = x[c] * alive
        loaded(9, 10)
        parts = split(x[...].reshape(192, 512), 0)
        layers = dot(parts, twice[...])
        for i in range(2):
            for f in range(6):
                cut = layers[192 * i:192 * i + 192, 128 * f:128 * f + 128]
                rows = slice(ROWS * i + 64 * f, ROWS * i + 64 * f + 64)
                table[rows, 0:128] = jnp.where(low_half, cut[0:64], cut[64:128]).astype(BF16)
                table[rows, 128:256] = cut[128:192].astype(BF16)

    def pack(buffer, q, rows):
        buffer[q, 0:64] = rows[:, 0:128]
        buffer[q, 64:96] = jnp.where(low_half, rows[0:32, 128:256], rows[32:64, 128:256])

    def unpack(message):
        tail = message[64:96]
        other = pltpu.roll(tail, 64, axis=1)
        third = jnp.concatenate([jnp.where(low_half, tail, other), jnp.where(low_half, other, tail)], axis=0)
        return jnp.concatenate([message[0:64], third], axis=1)

    def gather(i):
        lane_row = lane_iota((64, ROWS)).astype(F32)
        chosen = []
        for q in range(3 * i, 3 * i + 3):
            column = lists_in[q].T[0:64, 0:1]
            chosen.append(one_hot(lane_row == column))
        chosen = jnp.concatenate(chosen, axis=0)
        rows = dot(jnp.concatenate([chosen, chosen], axis=1), table[...])
        for n in range(3):
            q = 3 * i + n
            pack(frecv if q == SELF else fsend, q, rows[64 * n:64 * n + 64])

    def selection(i):
        a, b, c = (lists_in[q][0:1] for q in range(3 * i, 3 * i + 3))
        ids = [jnp.where(low_half, u, v) for u, v in ((a, b), (c, a), (b, c))]
        sel_t[i] = one_hot(row_iota((ROWS, ROWS)).astype(F32) == jnp.concatenate(ids, axis=1))

    def collect(i, weights, messages, first):
        rows = jnp.concatenate([unpack(messages[q]) for q in range(3 * i, 3 * i + 3)], axis=0)
        part = dot(weights[i], split(rows, 0))
        gathered[...] = part if first else gathered[...] + part

    lane = lane_iota((1, 128))
    ok_up2, ok_dn2 = (lane & 7) < 7, (lane & 7) > 0
    ok_up1, ok_dn1 = (lane & 63) < 56, (lane & 63) >= 8

    def step2(v):
        return jnp.where(ok_up2, pltpu.roll(v, 127, axis=1), 0.0) - jnp.where(ok_dn2, pltpu.roll(v, 1, axis=1), 0.0)

    def step1(v):
        return jnp.where(ok_up1, pltpu.roll(v, 120, axis=1), 0.0) - jnp.where(ok_dn1, pltpu.roll(v, 8, axis=1), 0.0)

    def step0(tiles):
        swung = [pltpu.roll(v, 64, axis=1) for v in tiles]
        none = jnp.zeros_like(swung[0])
        up = [jnp.where(low_half, swung[t], swung[t + 1] if t < 3 else none) for t in range(4)]
        dn = [jnp.where(low_half, swung[t - 1] if t > 0 else none, swung[t]) for t in range(4)]
        return [u - d for u, d in zip(up, dn)]

    def inner(i, _):
        rows = pl.ds(pl.multiple_of(i * 8, 8), 8)
        tiles = [[x[c, rows, 128 * t:128 * t + 128] for t in range(4)] for c in range(3)]
        first = [step0(tiles[c]) for c in range(3)]
        for t in range(4):
            cols = slice(128 * t, 128 * t + 128)
            d = [[first[c][t], step1(tiles[c][t]), step2(tiles[c][t])] for c in range(3)]
            for a in range(3):
                sym[a, rows, cols] = d[a][a]
                for b in range(a + 1, 3):
                    sym[pair(a, b), rows, cols] = d[a][b] + d[b][a]
            jac[rows, cols] = coef[1, rows] - coef[0, rows] * jnp.log(jac[rows, cols])
        return 0

    def by_quadrant(parts, weights):
        code = code_b[...]
        masks = [code == float(q) for q in range(5)]
        result = []
        for half in range(2):
            cut = slice(128 * half, 128 * half + 128)
            value = parts[:, cut]
            spread = dot(split(value, 1), weights[...])
            value = jnp.where(masks[4], value, 0.0)
            for q in range(4):
                value = jnp.where(masks[q], spread[:, 128 * q:128 * q + 128], value)
            result.append(value)
        return result

    def sided(parts, a, sign):
        low = [sign * part[128 * a:128 * a + 64] for part in parts]
        high = [part[128 * a + 64:128 * a + 128] for part in parts]
        return jnp.concatenate(
            [
                jnp.where(low_half, low[0], pltpu.roll(high[0], 64, axis=1)),
                jnp.where(low_half, pltpu.roll(low[0], 64, axis=1), high[0]),
                jnp.where(low_half, low[1], high[1]),
            ],
            axis=0,
        )

    def ghosts():
        parts = by_quadrant(gathered[...], fill)
        for a in range(3):
            sides = split(sided(parts, a, -1.0), 1)
            inj[a] = dot(sides, inject[256 * a:256 * a + 256]).reshape(3, 64, 512)

    def stress(i, _):
        rows = pl.ds(pl.multiple_of(i * 8, 8), 8)
        for t in range(4):
            cols = slice(128 * t, 128 * t + 128)
            shear = jac[rows, cols]
            diag = [sym[a, rows, cols] + inj[a, a, rows, cols] for a in range(3)]
            trace = coef[0, rows] * (diag[0] + diag[1] + diag[2])
            for a in range(3):
                sym[a, rows, cols] = trace + 2.0 * shear * diag[a]
                for b in range(a + 1, 3):
                    both = sym[pair(a, b), rows, cols] + inj[a, b, rows, cols] + inj[b, a, rows, cols]
                    sym[pair(a, b), rows, cols] = shear * both
        return 0

    def adjoint_faces():
        bars = []
        for a in range(3):
            stacked = jnp.concatenate([sym[pair(c, a)] for c in range(3)], axis=0)
            weights = twice[:, 256 * a:256 * a + 256]
            layers = dot(split(stacked, 1), jnp.concatenate([weights, weights], axis=0))
            for side in range(2):
                cut = layers[:, 128 * side:128 * side + 128]
                if side == 0:
                    cut = -cut
                bars.append(jnp.concatenate([jnp.where(low_half, cut[0:64], cut[64:128]), cut[128:192]], axis=1))
        parts = by_quadrant(jnp.concatenate(bars, axis=0), unfill)
        leaving[...] = split(jnp.concatenate(parts, axis=1), 0)

    def scatter(i):
        chosen = place[192 * i:192 * i + 192]
        rows = dot(jnp.concatenate([chosen, chosen], axis=1), leaving[...])
        for n in range(3):
            q = 3 * i + n
            pack(arecv if q == SELF else asend, q, rows[64 * n:64 * n + 64])

    def outer(i, _):
        rows = pl.ds(pl.multiple_of(i * 8, 8), 8)
        for c in range(3):
            first = step0([sym[pair(c, 0), rows, 128 * t:128 * t + 128] for t in range(4)])
            for t in range(4):
                cols = slice(128 * t, 128 * t + 128)
                back[c, rows, cols] = -(
                    first[t] + step1(sym[pair(c, 1), rows, cols]) + step2(sym[pair(c, 2), rows, cols])
                )
        return 0

    def land():
        rows = gathered[...]
        parts = [rows[:, 0:128], rows[:, 128:256]]
        sides = jnp.concatenate([split(sided(parts, a, 1.0), 1) for a in range(3)], axis=1)
        total = dot(sides, inject[...])
        alive = jnp.concatenate([coef[2]] * 4, axis=1)
        for c in range(3):
            out_ref[c] = (back[c] + total[64 * c:64 * c + 64]) * alive

    for load in loads:
        load.start()
    barrier = pltpu.get_barrier_semaphore()
    for q in OTHERS:
        guarded(q, lambda q=q: pl.semaphore_signal(barrier, inc=1, device_id=device(q), device_id_type=MESH))
    pl.when(jnp.logical_not(has_low))(lambda: clear(0))
    pl.when(jnp.logical_not(has_high))(lambda: clear(2))
    slot = request()
    pl.semaphore_wait(barrier, present)
    for q in OTHERS:
        send(q, lists, lists_in, list_ssem, list_rsem)
    lists_in[SELF] = lists[SELF]
    prepare(slot)

    for i in (2, 0, 1, 3):
        for q in range(3 * i, 3 * i + 3):
            if q != SELF:
                arrive(q, lists_in, list_ssem, list_rsem)
        gather(i)
        for q in range(3 * i, 3 * i + 3):
            if q != SELF:
                send(q, fsend, frecv, f_ssem, f_rsem)

    loaded(10, 11)
    lax.fori_loop(0, 8, inner, 0)
    for i in range(4):
        selection(i)
    loaded(11, 14)
    for n, i in enumerate(ARRIVALS):
        for q in range(3 * i, 3 * i + 3):
            if q != SELF:
                arrive(q, frecv, f_ssem, f_rsem)
        collect(i, place_t, frecv, n == 0)
    ghosts()
    lax.fori_loop(0, 8, stress, 0)
    adjoint_faces()
    for i in (2, 0, 1, 3):
        scatter(i)
        for q in range(3 * i, 3 * i + 3):
            if q != SELF:
                send(q, asend, arecv, a_ssem, a_rsem)

    lax.fori_loop(0, 8, outer, 0)
    for n, i in enumerate(ARRIVALS):
        for q in range(3 * i, 3 * i + 3):
            if q != SELF:
                arrive(q, arecv, a_ssem, a_rsem)
        collect(i, sel_t, arecv, n == 0)
    land()
    for q, copy in sends:
        guarded(q, copy.wait_send)


def per_device(
    direction, jacobian, shear_modulus, lame_modulus, refine_level, live_flag, neighbor, face_kind, face_quadrant
):
    ranges = lax.axis_size("morton")
    operands = [
        jnp.transpose(direction, (1, 0, 2)),
        jacobian,
        shear_modulus[None, :],
        lame_modulus[None, :],
        refine_level[None, :],
        live_flag[None, :],
        neighbor.T,
        face_kind.T,
        face_quadrant.T,
    ] + tables()
    buffers = [pltpu.VMEM(o.shape, o.dtype) for o in operands]
    operands = [pltpu.with_memory_space_constraint(o, pltpu.HBM) for o in operands]
    message = pltpu.VMEM((PEERS, 96, 128), F32)
    short = pltpu.VMEM((PEERS, 8, 128), F32)
    peers = pltpu.SemaphoreType.DMA((PEERS,))
    result = pl.pallas_call(
        functools.partial(kernel, ranges),
        out_shape=jax.ShapeDtypeStruct((3, BLOCKS, 512), F32),
        in_specs=[pl.BlockSpec(memory_space=pltpu.HBM)] * len(operands),
        out_specs=pl.BlockSpec(memory_space=pltpu.VMEM),
        scratch_shapes=buffers
        + [
            pltpu.VMEM((8, 128), F32),
            pltpu.VMEM((ROWS, 128), F32),
            pltpu.VMEM((3, 64, 128), F32),
            pltpu.VMEM((2 * ROWS, 256), BF16),
            pltpu.VMEM((4, ROWS, ROWS), BF16),
            pltpu.VMEM((SLOTS, ROWS), BF16),
            pltpu.VMEM((4, ROWS, ROWS), BF16),
            short,
            short,
            message,
            message,
            message,
            message,
            pltpu.VMEM((ROWS, 256), F32),
            pltpu.VMEM((2 * ROWS, 256), BF16),
            pltpu.VMEM((6, 64, 512), F32),
            pltpu.VMEM((3, 3, 64, 512), F32),
            pltpu.VMEM((3, 64, 512), F32),
            pltpu.SemaphoreType.DMA((len(operands),)),
            peers,
            peers,
            peers,
            peers,
            peers,
            peers,
        ],
        compiler_params=pltpu.CompilerParams(
            collective_id=0, has_side_effects=True, vmem_limit_bytes=48 * 1024 * 1024
        ),
        name="hessian_exchange",
    )(*operands)
    return jnp.transpose(result, (1, 0, 2))


def solution(mesh):
    in_specs = (
        P(("morton", "sub"), None, None),
        P(("morton", "sub"), None),
        P(("morton", "sub")),
        P(("morton", "sub")),
        P(("morton", "sub")),
        P(("morton", "sub")),
        P(("morton", "sub"), None),
        P(("morton", "sub"), None),
        P(("morton", "sub"), None),
    )
    out_specs = P(("morton", "sub"), None, None)
    return jax.shard_map(
        per_device, mesh=mesh, in_specs=in_specs, out_specs=out_specs, check_vma=False
    )
```

```python
import functools

import jax
import jax.numpy as jnp
import numpy as np
from jax import lax
from jax.experimental import pallas as pl
from jax.experimental.pallas import tpu as pltpu
from jax.sharding import PartitionSpec as P

BLOCKS = 64
ROWS = 6 * BLOCKS
PEERS = 12
SLOTS = PEERS * BLOCKS
F32 = jnp.float32
BF16 = jnp.bfloat16
MESH = pl.DeviceIdType.MESH
STEPS = (2, 1, 3, 0)
SELF = 7
OTHERS = tuple(q for q in range(PEERS) if q != SELF)
F_BATCHES = ((5, 6), (4, 7), (8, 9, 10, 11), (0, 1, 2, 3))
A_BATCHES = ((0, 1), (2, 3), (8, 9, 10, 11), (4, 5, 6, 7))
PAIRS = {(0, 0): 0, (1, 1): 1, (2, 2): 2, (0, 1): 3, (0, 2): 4, (1, 2): 5}


def pair(a, b):
    return PAIRS[(min(a, b), max(a, b))]


def mirror(q):
    return q - q % 4 + STEPS.index((4 - STEPS[q % 4]) % 4)


def tables():
    node = np.arange(512)
    coords = (node // 64, (node // 8) % 8, node % 8)
    pick = np.zeros((512, 6, 64), np.float32)
    for face in range(6):
        axis = face // 2
        others = [coords[a] for a in range(3) if a != axis]
        for n in np.nonzero(coords[axis] == 7 * (face % 2))[0]:
            pick[n, face, others[0][n] * 8 + others[1][n]] = 1
    halves = np.zeros((2, 8, 8), np.float32)
    for u in range(2):
        for i in range(8):
            halves[u, i, (7 * u + i) // 2] += 0.5
            halves[u, i, (7 * u + i + 1) // 2] += 0.5
    fill = np.zeros((128, 512), np.float32)
    unfill = np.zeros((128, 512), np.float32)
    for q in range(4):
        spread = np.kron(halves[q // 2], halves[q % 2])
        for half in range(2):
            lanes = slice(64 * half, 64 * half + 64)
            cols = slice(128 * q + 64 * half, 128 * q + 64 * half + 64)
            fill[lanes, cols] = spread.T
            unfill[lanes, cols] = spread
    twice = np.concatenate([pick, pick], axis=2).reshape(512, 768)
    inject = pick.reshape(512, 3, 128).transpose(1, 2, 0)[1:]
    inject = np.concatenate([inject, inject], axis=1).reshape(512, 512)
    before = np.triu(np.ones((ROWS, ROWS), np.float32), 1)
    stacked = (np.concatenate([t, t], axis=0) for t in (fill, unfill))
    return [jnp.asarray(t, BF16) for t in (twice, inject, *stacked, before)]


def split(values, axis):
    high = values.astype(BF16)
    low = (values - high.astype(F32)).astype(BF16)
    return jnp.concatenate([high, low], axis=axis)


def dot(a, b):
    return jnp.dot(a, b, preferred_element_type=F32)


def lane_iota(shape):
    return lax.broadcasted_iota(jnp.int32, shape, len(shape) - 1)


def row_iota(shape):
    return lax.broadcasted_iota(jnp.int32, shape, 0)


def one_hot(hits):
    return hits.astype(F32).astype(BF16)


def kernel(
    ranges,
    x_hbm, jac_hbm, mu_hbm, lam_hbm, level_hbm, live_hbm, nb_hbm, kind_hbm, quad_hbm,
    twice_hbm, inject_hbm, fill_hbm, unfill_hbm, before_hbm,
    out_ref,
    x, jac, mu, lam, level, live, nb, kind, quad,
    twice, inject, fill, unfill, before,
    tile_s, code_b, coef, table, sel_t, place, place_t, lists, lists_in,
    fsend, frecv, asend, arecv, gathered, leaving, sym, terms, edge, inj, back,
    in_sem, list_ssem, list_rsem, f_ssem, f_rsem, a_ssem, a_rsem,
):
    me_m = lax.axis_index("morton")
    me_x = lax.axis_index("sub")
    across = lax.rem(me_m, 2) * 2 - 1
    has_across = jnp.logical_and(me_m > 0, me_m < ranges - 1)
    present = 7 + 4 * has_across.astype(jnp.int32)
    low_half = lane_iota((1, 128)) < 64

    def device(q):
        return (me_m + across * (1 - q // 4), lax.rem(me_x + STEPS[q % 4], 4))

    def guarded(q, act):
        if q // 4 == 0:
            pl.when(has_across)(act)
        else:
            act()

    sends = []

    def send(q, src, dst, ssem, rsem):
        copy = pltpu.make_async_remote_copy(
            src_ref=src.at[q], dst_ref=dst.at[mirror(q)], send_sem=ssem.at[q], recv_sem=rsem.at[mirror(q)],
            device_id=device(q), device_id_type=MESH,
        )
        guarded(q, copy.start)
        sends.append((q, copy))

    def arrive(q, dst, ssem, rsem):
        copy = pltpu.make_async_remote_copy(
            src_ref=dst.at[q], dst_ref=dst.at[q], send_sem=ssem.at[q], recv_sem=rsem.at[q],
            device_id=device(q), device_id_type=MESH,
        )
        guarded(q, copy.wait_recv)

    loads = [
        pltpu.make_async_copy(src, dst, in_sem.at[i])
        for i, (src, dst) in enumerate(
            (
                (nb_hbm, nb), (before_hbm, before), (kind_hbm, kind), (quad_hbm, quad),
                (live_hbm, live), (mu_hbm, mu), (lam_hbm, lam), (level_hbm, level),
                (x_hbm, x), (twice_hbm, twice), (jac_hbm, jac), (inject_hbm, inject),
                (fill_hbm, fill), (unfill_hbm, unfill),
            )
        )
    ]

    def loaded(first, last):
        for load in loads[first:last]:
            load.wait()

    def clear():
        for q in range(4):
            frecv[q] = jnp.zeros((96, 128), F32)
            arecv[q] = jnp.zeros((96, 128), F32)
            lists_in[q] = jnp.zeros((8, 128), F32)

    def request():
        loaded(0, 2)
        tile_s[...] = jnp.zeros((8, 128), F32)
        want = nb[...]
        owner = want >> 6
        step = (owner - me_x) & 3
        place_of = jnp.where(step == 2, 0, jnp.where(step == 0, 3, jnp.where(step == 1, 1, 2)))
        peer = (1 - across * ((owner >> 2) - me_m)) * 4 + place_of
        opposite = row_iota((6, 64)) ^ 1
        tile_s[0:6, 0:64] = (peer * 512 + opposite * 64 + (want & 63)).astype(F32)
        packed = tile_s[...]
        turned = pltpu.roll(packed, 64, axis=1)
        pairs = [jnp.where(low_half, packed[f:f + 1], turned[f + 1:f + 2]) for f in (0, 2, 4)]
        row = jnp.concatenate(pairs, axis=1).astype(jnp.int32)
        ident = row & 511
        hits = row_iota((16, ROWS)) == (row >> 9)
        rank = dot(one_hot(hits), before[...])
        base = (row_iota((16, ROWS)) * 64).astype(F32)
        slot = jnp.sum(jnp.where(hits, rank + base, 0.0), axis=0, keepdims=True)
        place[...] = one_hot(row_iota((SLOTS, ROWS)).astype(F32) == slot)
        which = row_iota((8, ROWS))
        parts = jnp.where(which == 0, ident & 63, jnp.where(which == 1, ident >> 6, 0))
        found = lax.dot_general(
            parts.astype(F32).astype(BF16), place[...], (((1,), (1,)), ((), ())), preferred_element_type=F32
        )
        codes = jnp.broadcast_to(found[0:1] + 64.0 * found[1:2], (8, SLOTS))
        for t in range(PEERS // 2):
            both = codes[:, 128 * t:128 * t + 128]
            swapped = pltpu.roll(both, 64, axis=1)
            lists[2 * t] = jnp.where(low_half, both, swapped)
            lists[2 * t + 1] = jnp.where(low_half, swapped, both)
        return slot

    def prepare(slot):
        slot_col = jnp.broadcast_to(slot, (8, ROWS)).T[:, 0:1]
        lanes = (lane_iota((ROWS, 512)) & 255).astype(F32)
        for i in range(3):
            place_t[i] = one_hot(lanes == slot_col - 256.0 * i)
        loaded(2, 8)
        scale = jnp.left_shift(jnp.ones((1, 64), jnp.int32), level[...]).astype(F32) * 0.25
        tile_s[...] = jnp.zeros((8, 128), F32)
        tile_s[0:1, 0:64] = lam[...] * scale * scale
        tile_s[1:2, 0:64] = mu[...] * scale * scale
        tile_s[2:3, 0:64] = live[...].astype(F32)
        flat = tile_s[...].T
        for i in range(3):
            coef[i] = jnp.broadcast_to(flat[0:64, i:i + 1], (64, 128))
        tile_s[...] = jnp.zeros((8, 128), F32)
        kinds = kind[...]
        tile_s[0:6, 0:64] = jnp.where(kinds == 1, 4, jnp.where(kinds == 2, quad[...], -1)).astype(F32)
        flat = tile_s[...].T
        for f in range(6):
            code_b[64 * f:64 * f + 64] = jnp.broadcast_to(flat[0:64, f:f + 1], (64, 128))
        loaded(8, 9)
        alive = jnp.concatenate([coef[2]] * 4, axis=1)
        for c in range(3):
            x[c] = x[c] * alive
        loaded(9, 10)
        parts = split(x[...].reshape(192, 512), 0)
        layers = dot(parts, twice[...])
        for i in range(2):
            for f in range(6):
                cut = layers[192 * i:192 * i + 192, 128 * f:128 * f + 128]
                rows = slice(ROWS * i + 64 * f, ROWS * i + 64 * f + 64)
                table[rows, 0:128] = jnp.where(low_half, cut[0:64], cut[64:128]).astype(BF16)
                table[rows, 128:256] = cut[128:192].astype(BF16)

    def pack(buffer, q, rows):
        buffer[q, 0:64] = rows[:, 0:128]
        buffer[q, 64:96] = jnp.where(low_half, rows[0:32, 128:256], rows[32:64, 128:256])

    def unpack(message):
        tail = message[64:96]
        other = pltpu.roll(tail, 64, axis=1)
        third = jnp.concatenate([jnp.where(low_half, tail, other), jnp.where(low_half, other, tail)], axis=0)
        return jnp.concatenate([message[0:64], third], axis=1)

    def gather(batch):
        lane_row = lane_iota((64, ROWS)).astype(F32)
        chosen = []
        for q in batch:
            column = lists_in[q].T[0:64, 0:1]
            chosen.append(one_hot(lane_row == column))
        chosen = jnp.concatenate(chosen, axis=0)
        rows = dot(jnp.concatenate([chosen, chosen], axis=1), table[...])
        for n, q in enumerate(batch):
            pack(frecv if q == SELF else fsend, q, rows[64 * n:64 * n + 64])

    def selection(i):
        a, b, c, d = (lists_in[q][0:1] for q in range(4 * i, 4 * i + 4))
        ids = [jnp.where(low_half, a, b), jnp.where(low_half, c, d)] * 2
        sel_t[i] = one_hot(row_iota((ROWS, 512)).astype(F32) == jnp.concatenate(ids, axis=1))

    def collect(i, weights, messages, first):
        rows = jnp.concatenate([unpack(messages[q]) for q in range(4 * i, 4 * i + 4)], axis=0)
        part = dot(weights[i], split(rows, 0))
        gathered[...] = part if first else gathered[...] + part

    lane = lane_iota((1, 128))
    ok_up2, ok_dn2 = (lane & 7) < 7, (lane & 7) > 0
    ok_up1, ok_dn1 = (lane & 63) < 56, (lane & 63) >= 8

    def step2(v):
        return jnp.where(ok_up2, pltpu.roll(v, 127, axis=1), 0.0) - jnp.where(ok_dn2, pltpu.roll(v, 1, axis=1), 0.0)

    def step1(v):
        return jnp.where(ok_up1, pltpu.roll(v, 120, axis=1), 0.0) - jnp.where(ok_dn1, pltpu.roll(v, 8, axis=1), 0.0)

    def step0(tiles):
        swung = [pltpu.roll(v, 64, axis=1) for v in tiles]
        none = jnp.zeros_like(swung[0])
        up = [jnp.where(low_half, swung[t], swung[t + 1] if t < 3 else none) for t in range(4)]
        dn = [jnp.where(low_half, swung[t - 1] if t > 0 else none, swung[t]) for t in range(4)]
        return [u - d for u, d in zip(up, dn)]

    def inner(i, _):
        rows = pl.ds(pl.multiple_of(i * 8, 8), 8)
        tiles = [[x[c, rows, 128 * t:128 * t + 128] for t in range(4)] for c in range(3)]
        first = [step0(tiles[c]) for c in range(3)]
        for t in range(4):
            cols = slice(128 * t, 128 * t + 128)
            d = [[first[c][t], step1(tiles[c][t]), step2(tiles[c][t])] for c in range(3)]
            for a in range(3):
                sym[a, rows, cols] = d[a][a]
                for b in range(a + 1, 3):
                    sym[pair(a, b), rows, cols] = d[a][b] + d[b][a]
            jac[rows, cols] = coef[1, rows] - coef[0, rows] * jnp.log(jac[rows, cols])
        return 0

    def by_quadrant(parts, weights):
        code = code_b[...]
        masks = [code == float(q) for q in range(5)]
        result = []
        for half in range(2):
            cut = slice(128 * half, 128 * half + 128)
            value = parts[:, cut]
            spread = dot(split(value, 1), weights[...])
            value = jnp.where(masks[4], value, 0.0)
            for q in range(4):
                value = jnp.where(masks[q], spread[:, 128 * q:128 * q + 128], value)
            result.append(value)
        return result

    def sided(parts, a, sign):
        low = [sign * part[128 * a:128 * a + 64] for part in parts]
        high = [part[128 * a + 64:128 * a + 128] for part in parts]
        return jnp.concatenate(
            [
                jnp.where(low_half, low[0], pltpu.roll(high[0], 64, axis=1)),
                jnp.where(low_half, pltpu.roll(low[0], 64, axis=1), high[0]),
                jnp.where(low_half, low[1], high[1]),
            ],
            axis=0,
        )

    def ghosts():
        parts = by_quadrant(gathered[...], fill)
        edge[...] = sided(parts, 0, -1.0).reshape(3, 64, 128)
        for a in (1, 2):
            sides = split(sided(parts, a, -1.0), 1)
            inj[a - 1] = dot(sides, inject[256 * a - 256:256 * a]).reshape(3, 64, 512)

    def at_ends(v, t):
        return jnp.where(low_half, v, 0.0) if t == 0 else jnp.where(low_half, 0.0, v)

    def stress(i, _):
        rows = pl.ds(pl.multiple_of(i * 16, 16), 16)
        for t in range(4):
            cols = slice(128 * t, 128 * t + 128)
            shear = jac[rows, cols]
            e = [sym[k, rows, cols] for k in range(6)]
            if t in (0, 3):
                for c in range(3):
                    e[pair(c, 0)] = e[pair(c, 0)] + at_ends(edge[c, rows], t)
            for a in (1, 2):
                for c in range(3):
                    e[pair(c, a)] = e[pair(c, a)] + inj[a - 1, c, rows, cols]
            trace = coef[0, rows] * (e[0] + e[1] + e[2])
            for k in range(6):
                value = trace + 2.0 * shear * e[k] if k < 3 else shear * e[k]
                sym[k, rows, cols] = value
                if k > 0:
                    high = value.astype(BF16)
                    terms[0, k - 1, rows, cols] = high
                    terms[1, k - 1, rows, cols] = (value - high.astype(F32)).astype(BF16)
        return 0

    def adjoint_faces():
        first = [sym[pair(c, 0), :, 0:128] for c in range(3)]
        last = [sym[pair(c, 0), :, 384:512] for c in range(3)]

        def swing(v):
            return pltpu.roll(v, 64, axis=1)

        bars = [
            jnp.concatenate(
                [-jnp.where(low_half, first[0], swing(first[1])), -jnp.where(low_half, first[2], swing(first[2]))], axis=1
            ),
            jnp.concatenate(
                [jnp.where(low_half, swing(last[0]), last[1]), jnp.where(low_half, swing(last[2]), last[2])], axis=1
            ),
        ]
        for a in (1, 2):
            stacked = [terms[part, pair(c, a) - 1] for part in range(2) for c in range(3)]
            layers = dot(jnp.concatenate(stacked, axis=0), twice[:, 256 * a:256 * a + 256])
            layers = layers[0:192] + layers[192:384]
            for side in range(2):
                cut = layers[:, 128 * side:128 * side + 128]
                if side == 0:
                    cut = -cut
                bars.append(jnp.concatenate([jnp.where(low_half, cut[0:64], cut[64:128]), cut[128:192]], axis=1))
        parts = by_quadrant(jnp.concatenate(bars, axis=0), unfill)
        leaving[...] = split(jnp.concatenate(parts, axis=1), 0)

    def scatter(batch):
        chosen = place[64 * batch[0]:64 * batch[-1] + 64]
        rows = dot(jnp.concatenate([chosen, chosen], axis=1), leaving[...])
        for n, q in enumerate(batch):
            pack(arecv if q == SELF else asend, q, rows[64 * n:64 * n + 64])

    def outer(i, _):
        rows = pl.ds(pl.multiple_of(i * 8, 8), 8)
        for c in range(3):
            first = step0([sym[pair(c, 0), rows, 128 * t:128 * t + 128] for t in range(4)])
            for t in range(4):
                cols = slice(128 * t, 128 * t + 128)
                back[c, rows, cols] = -(
                    first[t] + step1(sym[pair(c, 1), rows, cols]) + step2(sym[pair(c, 2), rows, cols])
                )
        return 0

    def land():
        rows = gathered[...]
        parts = [rows[:, 0:128], rows[:, 128:256]]
        ends = sided(parts, 0, 1.0)
        sides = split(jnp.concatenate([sided(parts, a, 1.0) for a in (1, 2)], axis=1), 0)
        total = dot(sides, jnp.concatenate([inject[0:128], inject[256:384]], axis=0))
        for c in range(3):
            for t in range(4):
                cols = slice(128 * t, 128 * t + 128)
                value = back[c, :, cols] + (total[64 * c:64 * c + 64, cols] + total[192 + 64 * c:256 + 64 * c, cols])
                if t in (0, 3):
                    value = value + at_ends(ends[64 * c:64 * c + 64], t)
                out_ref[c, :, cols] = value * coef[2]

    for load in loads:
        load.start()
    barrier = pltpu.get_barrier_semaphore()
    for q in OTHERS:
        guarded(q, lambda q=q: pl.semaphore_signal(barrier, inc=1, device_id=device(q), device_id_type=MESH))
    pl.when(jnp.logical_not(has_across))(clear)
    slot = request()
    pl.semaphore_wait(barrier, present)
    for q in OTHERS:
        send(q, lists, lists_in, list_ssem, list_rsem)
    lists_in[SELF] = lists[SELF]
    prepare(slot)

    for batch in F_BATCHES:
        for q in batch:
            if q != SELF:
                arrive(q, lists_in, list_ssem, list_rsem)
        gather(batch)
        for q in batch:
            if q != SELF:
                send(q, fsend, frecv, f_ssem, f_rsem)

    loaded(10, 11)
    lax.fori_loop(0, 8, inner, 0)
    for i in range(3):
        selection(i)
    loaded(11, 14)
    for n, i in enumerate((1, 0, 2)):
        for q in range(4 * i, 4 * i + 4):
            if q != SELF:
                arrive(q, frecv, f_ssem, f_rsem)
        collect(i, place_t, frecv, n == 0)
    ghosts()
    lax.fori_loop(0, 4, stress, 0)
    adjoint_faces()
    for batch in A_BATCHES:
        scatter(batch)
        for q in batch:
            if q != SELF:
                send(q, asend, arecv, a_ssem, a_rsem)

    lax.fori_loop(0, 8, outer, 0)
    for n, i in enumerate((0, 1, 2)):
        for q in range(4 * i, 4 * i + 4):
            if q != SELF:
                arrive(q, arecv, a_ssem, a_rsem)
        collect(i, sel_t, arecv, n == 0)
    land()
    for q, copy in sends:
        guarded(q, copy.wait_send)


def per_device(
    direction, jacobian, shear_modulus, lame_modulus, refine_level, live_flag, neighbor, face_kind, face_quadrant
):
    ranges = lax.axis_size("morton")
    operands = [
        jnp.transpose(direction, (1, 0, 2)),
        jacobian,
        shear_modulus[None, :],
        lame_modulus[None, :],
        refine_level[None, :],
        live_flag[None, :],
        neighbor.T,
        face_kind.T,
        face_quadrant.T,
    ] + tables()
    buffers = [pltpu.VMEM(o.shape, o.dtype) for o in operands]
    operands = [pltpu.with_memory_space_constraint(o, pltpu.HBM) for o in operands]
    message = pltpu.VMEM((PEERS, 96, 128), F32)
    short = pltpu.VMEM((PEERS, 8, 128), F32)
    peers = pltpu.SemaphoreType.DMA((PEERS,))
    result = pl.pallas_call(
        functools.partial(kernel, ranges),
        out_shape=jax.ShapeDtypeStruct((3, BLOCKS, 512), F32),
        in_specs=[pl.BlockSpec(memory_space=pltpu.HBM)] * len(operands),
        out_specs=pl.BlockSpec(memory_space=pltpu.VMEM),
        scratch_shapes=buffers
        + [
            pltpu.VMEM((8, 128), F32),
            pltpu.VMEM((ROWS, 128), F32),
            pltpu.VMEM((3, 64, 128), F32),
            pltpu.VMEM((2 * ROWS, 256), BF16),
            pltpu.VMEM((3, ROWS, 512), BF16),
            pltpu.VMEM((SLOTS, ROWS), BF16),
            pltpu.VMEM((3, ROWS, 512), BF16),
            short,
            short,
            message,
            message,
            message,
            message,
            pltpu.VMEM((ROWS, 256), F32),
            pltpu.VMEM((2 * ROWS, 256), BF16),
            pltpu.VMEM((6, 64, 512), F32),
            pltpu.VMEM((2, 5, 64, 512), BF16),
            pltpu.VMEM((3, 64, 128), F32),
            pltpu.VMEM((2, 3, 64, 512), F32),
            pltpu.VMEM((3, 64, 512), F32),
            pltpu.SemaphoreType.DMA((len(operands),)),
            peers,
            peers,
            peers,
            peers,
            peers,
            peers,
        ],
        compiler_params=pltpu.CompilerParams(
            collective_id=0, has_side_effects=True, vmem_limit_bytes=48 * 1024 * 1024
        ),
        name="hessian_exchange",
    )(*operands)
    return jnp.transpose(result, (1, 0, 2))


def solution(mesh):
    in_specs = (
        P(("morton", "sub"), None, None),
        P(("morton", "sub"), None),
        P(("morton", "sub")),
        P(("morton", "sub")),
        P(("morton", "sub")),
        P(("morton", "sub")),
        P(("morton", "sub"), None),
        P(("morton", "sub"), None),
        P(("morton", "sub"), None),
    )
    out_specs = P(("morton", "sub"), None, None)
    return jax.shard_map(
        per_device, mesh=mesh, in_specs=in_specs, out_specs=out_specs, check_vma=False
    )
```

```python
import functools

import jax
import jax.numpy as jnp
import numpy as np
from jax import lax
from jax.experimental import pallas as pl
from jax.experimental.pallas import tpu as pltpu
from jax.sharding import PartitionSpec as P

BLOCKS = 64
ROWS = 6 * BLOCKS
PEERS = 12
SLOTS = PEERS * BLOCKS
F32 = jnp.float32
BF16 = jnp.bfloat16
MESH = pl.DeviceIdType.MESH
STEPS = (2, 1, 3, 0)
SELF = 7
OTHERS = tuple(q for q in range(PEERS) if q != SELF)
F_BATCHES = ((5, 6), (4, 7), (8, 9, 10, 11), (0, 1, 2, 3))
A_BATCHES = ((0, 1), (2, 3), (8, 9, 10, 11), (4, 5, 6, 7))
PAIRS = {(0, 0): 0, (1, 1): 1, (2, 2): 2, (0, 1): 3, (0, 2): 4, (1, 2): 5}


def pair(a, b):
    return PAIRS[(min(a, b), max(a, b))]


def mirror(q):
    return q - q % 4 + STEPS.index((4 - STEPS[q % 4]) % 4)


def tables():
    node = np.arange(512)
    coords = (node // 64, (node // 8) % 8, node % 8)
    pick = np.zeros((512, 6, 64), np.float32)
    for face in range(6):
        axis = face // 2
        others = [coords[a] for a in range(3) if a != axis]
        for n in np.nonzero(coords[axis] == 7 * (face % 2))[0]:
            pick[n, face, others[0][n] * 8 + others[1][n]] = 1
    halves = np.zeros((2, 8, 8), np.float32)
    for u in range(2):
        for i in range(8):
            halves[u, i, (7 * u + i) // 2] += 0.5
            halves[u, i, (7 * u + i + 1) // 2] += 0.5
    fill = np.zeros((128, 512), np.float32)
    unfill = np.zeros((128, 512), np.float32)
    for q in range(4):
        spread = np.kron(halves[q // 2], halves[q % 2])
        for half in range(2):
            lanes = slice(64 * half, 64 * half + 64)
            cols = slice(128 * q + 64 * half, 128 * q + 64 * half + 64)
            fill[lanes, cols] = spread.T
            unfill[lanes, cols] = spread
    twice = np.concatenate([pick, pick], axis=2).reshape(512, 768)
    inject = pick.reshape(512, 3, 128).transpose(1, 2, 0)[1:]
    inject = np.concatenate([inject, inject], axis=1).reshape(512, 512)
    before = np.triu(np.ones((ROWS, ROWS), np.float32), 1)
    stacked = (np.concatenate([t, t], axis=0) for t in (fill, unfill))
    return [jnp.asarray(t, BF16) for t in (twice, inject, *stacked, before)]


def split(values, axis):
    high = values.astype(BF16)
    low = (values - high.astype(F32)).astype(BF16)
    return jnp.concatenate([high, low], axis=axis)


def dot(a, b):
    return jnp.dot(a, b, preferred_element_type=F32)


def lane_iota(shape):
    return lax.broadcasted_iota(jnp.int32, shape, len(shape) - 1)


def row_iota(shape):
    return lax.broadcasted_iota(jnp.int32, shape, 0)


def one_hot(hits):
    return hits.astype(F32).astype(BF16)


def kernel(
    ranges,
    x_hbm, jac_hbm, mu_hbm, lam_hbm, level_hbm, live_hbm, nb_hbm, kind_hbm, quad_hbm,
    twice_hbm, inject_hbm, fill_hbm, unfill_hbm, before_hbm,
    out_ref,
    x, jac, mu, lam, level, live, nb, kind, quad,
    twice, inject, fill, unfill, before,
    tile_s, code_b, coef, table, sel_t, place, place_t, lists, lists_in,
    fsend, frecv, asend, arecv, gathered, leaving, sym, terms, edge, inj, back,
    in_sem, list_ssem, list_rsem, f_ssem, f_rsem, a_ssem, a_rsem,
):
    me_m = lax.axis_index("morton")
    me_x = lax.axis_index("sub")
    across = lax.rem(me_m, 2) * 2 - 1
    has_across = jnp.logical_and(me_m > 0, me_m < ranges - 1)
    present = 7 + 4 * has_across.astype(jnp.int32)
    low_half = lane_iota((1, 128)) < 64

    def device(q):
        return (me_m + across * (1 - q // 4), lax.rem(me_x + STEPS[q % 4], 4))

    def guarded(q, act):
        if q // 4 == 0:
            pl.when(has_across)(act)
        else:
            act()

    sends = []

    def send(q, src, dst, ssem, rsem, rows=96):
        copy = pltpu.make_async_remote_copy(
            src_ref=src.at[q, 0:rows], dst_ref=dst.at[mirror(q), 0:rows], send_sem=ssem.at[q], recv_sem=rsem.at[mirror(q)],
            device_id=device(q), device_id_type=MESH,
        )
        guarded(q, copy.start)
        sends.append((q, copy))

    def arrive(q, dst, ssem, rsem, rows=96):
        copy = pltpu.make_async_remote_copy(
            src_ref=dst.at[q, 0:rows], dst_ref=dst.at[q, 0:rows], send_sem=ssem.at[q], recv_sem=rsem.at[q],
            device_id=device(q), device_id_type=MESH,
        )
        guarded(q, copy.wait_recv)

    loads = [
        pltpu.make_async_copy(src, dst, in_sem.at[i])
        for i, (src, dst) in enumerate(
            (
                (nb_hbm, nb), (before_hbm, before), (kind_hbm, kind), (quad_hbm, quad),
                (live_hbm, live), (mu_hbm, mu), (lam_hbm, lam), (level_hbm, level),
                (x_hbm, x), (twice_hbm, twice), (jac_hbm, jac), (inject_hbm, inject),
                (fill_hbm, fill), (unfill_hbm, unfill),
            )
        )
    ]

    def loaded(first, last):
        for load in loads[first:last]:
            load.wait()

    def clear():
        for q in range(4):
            frecv[q] = jnp.zeros((96, 128), F32)
            arecv[q] = jnp.zeros((96, 128), F32)
            lists_in[q] = jnp.zeros((8, 128), F32)

    def request():
        loaded(0, 2)
        tile_s[...] = jnp.zeros((8, 128), F32)
        want = nb[...]
        owner = want >> 6
        step = (owner - me_x) & 3
        place_of = jnp.where(step == 2, 0, jnp.where(step == 0, 3, jnp.where(step == 1, 1, 2)))
        peer = (1 - across * ((owner >> 2) - me_m)) * 4 + place_of
        opposite = row_iota((6, 64)) ^ 1
        tile_s[0:6, 0:64] = (peer * 512 + opposite * 64 + (want & 63)).astype(F32)
        packed = tile_s[...]
        turned = pltpu.roll(packed, 64, axis=1)
        pairs = [jnp.where(low_half, packed[f:f + 1], turned[f + 1:f + 2]) for f in (0, 2, 4)]
        row = jnp.concatenate(pairs, axis=1).astype(jnp.int32)
        ident = row & 511
        hits = row_iota((16, ROWS)) == (row >> 9)
        rank = dot(one_hot(hits), before[...])
        base = (row_iota((16, ROWS)) * 64).astype(F32)
        slot = jnp.sum(jnp.where(hits, rank + base, 0.0), axis=0, keepdims=True)
        place[...] = one_hot(row_iota((SLOTS, ROWS)).astype(F32) == slot)
        which = row_iota((8, ROWS))
        parts = jnp.where(which == 0, ident & 63, jnp.where(which == 1, ident >> 6, 0))
        found = lax.dot_general(
            parts.astype(F32).astype(BF16), place[...], (((1,), (1,)), ((), ())), preferred_element_type=F32
        )
        codes = jnp.broadcast_to(found[0:1] + 64.0 * found[1:2], (8, SLOTS))
        for t in range(PEERS // 2):
            both = codes[:, 128 * t:128 * t + 128]
            swapped = pltpu.roll(both, 64, axis=1)
            lists[2 * t] = jnp.where(low_half, both, swapped)
            lists[2 * t + 1] = jnp.where(low_half, swapped, both)
        return slot

    def prepare(slot):
        slot_col = jnp.broadcast_to(slot, (8, ROWS)).T[:, 0:1]
        lanes = (lane_iota((ROWS, 512)) & 255).astype(F32)
        for i in range(3):
            place_t[i] = one_hot(lanes == slot_col - 256.0 * i)
        loaded(2, 8)
        scale = jnp.left_shift(jnp.ones((1, 64), jnp.int32), level[...]).astype(F32) * 0.25
        tile_s[...] = jnp.zeros((8, 128), F32)
        tile_s[0:1, 0:64] = lam[...] * scale * scale
        tile_s[1:2, 0:64] = mu[...] * scale * scale
        tile_s[2:3, 0:64] = live[...].astype(F32)
        flat = tile_s[...].T
        for i in range(3):
            coef[i] = jnp.broadcast_to(flat[0:64, i:i + 1], (64, 128))
        tile_s[...] = jnp.zeros((8, 128), F32)
        kinds = kind[...]
        tile_s[0:6, 0:64] = jnp.where(kinds == 1, 4, jnp.where(kinds == 2, quad[...], -1)).astype(F32)
        flat = tile_s[...].T
        for f in range(6):
            code_b[64 * f:64 * f + 64] = jnp.broadcast_to(flat[0:64, f:f + 1], (64, 128))
        loaded(8, 9)
        alive = jnp.concatenate([coef[2]] * 4, axis=1)
        for c in range(3):
            x[c] = x[c] * alive
        loaded(9, 10)
        parts = split(x[...].reshape(192, 512), 0)
        layers = dot(parts, twice[...])
        for i in range(2):
            for f in range(6):
                cut = layers[192 * i:192 * i + 192, 128 * f:128 * f + 128]
                rows = slice(ROWS * i + 64 * f, ROWS * i + 64 * f + 64)
                table[rows, 0:128] = jnp.where(low_half, cut[0:64], cut[64:128]).astype(BF16)
                table[rows, 128:256] = cut[128:192].astype(BF16)

    def pack(buffer, q, rows):
        buffer[q, 0:64] = rows[:, 0:128]
        buffer[q, 64:96] = jnp.where(low_half, rows[0:32, 128:256], rows[32:64, 128:256])

    def unpack(message):
        tail = message[64:96]
        other = pltpu.roll(tail, 64, axis=1)
        third = jnp.concatenate([jnp.where(low_half, tail, other), jnp.where(low_half, other, tail)], axis=0)
        return jnp.concatenate([message[0:64], third], axis=1)

    def gather(batch):
        lane_row = lane_iota((64, ROWS)).astype(F32)
        chosen = []
        for q in batch:
            column = jnp.broadcast_to(lists_in[q, 0:1], (8, 128)).T[0:64, 0:1]
            chosen.append(one_hot(lane_row == column))
        chosen = jnp.concatenate(chosen, axis=0)
        rows = dot(jnp.concatenate([chosen, chosen], axis=1), table[...])
        for n, q in enumerate(batch):
            pack(frecv if q == SELF else fsend, q, rows[64 * n:64 * n + 64])

    def selection(i):
        a, b, c, d = (lists_in[q, 0:1] for q in range(4 * i, 4 * i + 4))
        ids = [jnp.where(low_half, a, b), jnp.where(low_half, c, d)] * 2
        sel_t[i] = one_hot(row_iota((ROWS, 512)).astype(F32) == jnp.concatenate(ids, axis=1))

    def collect(i, weights, messages, first):
        rows = jnp.concatenate([unpack(messages[q]) for q in range(4 * i, 4 * i + 4)], axis=0)
        part = dot(weights[i], split(rows, 0))
        gathered[...] = part if first else gathered[...] + part

    lane = lane_iota((1, 128))
    ok_up2, ok_dn2 = (lane & 7) < 7, (lane & 7) > 0
    ok_up1, ok_dn1 = (lane & 63) < 56, (lane & 63) >= 8

    def step2(v):
        return jnp.where(ok_up2, pltpu.roll(v, 127, axis=1), 0.0) - jnp.where(ok_dn2, pltpu.roll(v, 1, axis=1), 0.0)

    def step1(v):
        return jnp.where(ok_up1, pltpu.roll(v, 120, axis=1), 0.0) - jnp.where(ok_dn1, pltpu.roll(v, 8, axis=1), 0.0)

    def step0(tiles):
        swung = [pltpu.roll(v, 64, axis=1) for v in tiles]
        none = jnp.zeros_like(swung[0])
        up = [jnp.where(low_half, swung[t], swung[t + 1] if t < 3 else none) for t in range(4)]
        dn = [jnp.where(low_half, swung[t - 1] if t > 0 else none, swung[t]) for t in range(4)]
        return [u - d for u, d in zip(up, dn)]

    def inner(i, _):
        rows = pl.ds(pl.multiple_of(i * 8, 8), 8)
        tiles = [[x[c, rows, 128 * t:128 * t + 128] for t in range(4)] for c in range(3)]
        first = [step0(tiles[c]) for c in range(3)]
        for t in range(4):
            cols = slice(128 * t, 128 * t + 128)
            d = [[first[c][t], step1(tiles[c][t]), step2(tiles[c][t])] for c in range(3)]
            for a in range(3):
                sym[a, rows, cols] = d[a][a]
                for b in range(a + 1, 3):
                    sym[pair(a, b), rows, cols] = d[a][b] + d[b][a]
            jac[rows, cols] = coef[1, rows] - coef[0, rows] * jnp.log(jac[rows, cols])
        return 0

    def by_quadrant(parts, weights):
        code = code_b[...]
        masks = [code == float(q) for q in range(5)]
        result = []
        for half in range(2):
            cut = slice(128 * half, 128 * half + 128)
            value = parts[:, cut]
            spread = dot(split(value, 1), weights[...])
            value = jnp.where(masks[4], value, 0.0)
            for q in range(4):
                value = jnp.where(masks[q], spread[:, 128 * q:128 * q + 128], value)
            result.append(value)
        return result

    def sided(parts, a, sign):
        low = [sign * part[128 * a:128 * a + 64] for part in parts]
        high = [part[128 * a + 64:128 * a + 128] for part in parts]
        return jnp.concatenate(
            [
                jnp.where(low_half, low[0], pltpu.roll(high[0], 64, axis=1)),
                jnp.where(low_half, pltpu.roll(low[0], 64, axis=1), high[0]),
                jnp.where(low_half, low[1], high[1]),
            ],
            axis=0,
        )

    def ghosts():
        parts = by_quadrant(gathered[...], fill)
        edge[...] = sided(parts, 0, -1.0).reshape(3, 64, 128)
        for a in (1, 2):
            sides = split(sided(parts, a, -1.0), 1)
            inj[a - 1] = dot(sides, inject[256 * a - 256:256 * a]).reshape(3, 64, 512)

    def at_ends(v, t):
        return jnp.where(low_half, v, 0.0) if t == 0 else jnp.where(low_half, 0.0, v)

    def stress(i, _):
        rows = pl.ds(pl.multiple_of(i * 16, 16), 16)
        for t in range(4):
            cols = slice(128 * t, 128 * t + 128)
            shear = jac[rows, cols]
            e = [sym[k, rows, cols] for k in range(6)]
            if t in (0, 3):
                for c in range(3):
                    e[pair(c, 0)] = e[pair(c, 0)] + at_ends(edge[c, rows], t)
            for a in (1, 2):
                for c in range(3):
                    e[pair(c, a)] = e[pair(c, a)] + inj[a - 1, c, rows, cols]
            trace = coef[0, rows] * (e[0] + e[1] + e[2])
            for k in range(6):
                value = trace + 2.0 * shear * e[k] if k < 3 else shear * e[k]
                sym[k, rows, cols] = value
                if k > 0:
                    high = value.astype(BF16)
                    terms[0, k - 1, rows, cols] = high
                    terms[1, k - 1, rows, cols] = (value - high.astype(F32)).astype(BF16)
        return 0

    def adjoint_faces():
        first = [sym[pair(c, 0), :, 0:128] for c in range(3)]
        last = [sym[pair(c, 0), :, 384:512] for c in range(3)]

        def swing(v):
            return pltpu.roll(v, 64, axis=1)

        bars = [
            jnp.concatenate(
                [-jnp.where(low_half, first[0], swing(first[1])), -jnp.where(low_half, first[2], swing(first[2]))], axis=1
            ),
            jnp.concatenate(
                [jnp.where(low_half, swing(last[0]), last[1]), jnp.where(low_half, swing(last[2]), last[2])], axis=1
            ),
        ]
        for a in (1, 2):
            stacked = [terms[part, pair(c, a) - 1] for part in range(2) for c in range(3)]
            layers = dot(jnp.concatenate(stacked, axis=0), twice[:, 256 * a:256 * a + 256])
            layers = layers[0:192] + layers[192:384]
            for side in range(2):
                cut = layers[:, 128 * side:128 * side + 128]
                if side == 0:
                    cut = -cut
                bars.append(jnp.concatenate([jnp.where(low_half, cut[0:64], cut[64:128]), cut[128:192]], axis=1))
        parts = by_quadrant(jnp.concatenate(bars, axis=0), unfill)
        leaving[...] = split(jnp.concatenate(parts, axis=1), 0)

    def scatter(batch):
        chosen = place[64 * batch[0]:64 * batch[-1] + 64]
        rows = dot(jnp.concatenate([chosen, chosen], axis=1), leaving[...])
        for n, q in enumerate(batch):
            pack(arecv if q == SELF else asend, q, rows[64 * n:64 * n + 64])

    def outer(i, _):
        rows = pl.ds(pl.multiple_of(i * 8, 8), 8)
        for c in range(3):
            first = step0([sym[pair(c, 0), rows, 128 * t:128 * t + 128] for t in range(4)])
            for t in range(4):
                cols = slice(128 * t, 128 * t + 128)
                back[c, rows, cols] = -(
                    first[t] + step1(sym[pair(c, 1), rows, cols]) + step2(sym[pair(c, 2), rows, cols])
                )
        return 0

    def land():
        rows = gathered[...]
        parts = [rows[:, 0:128], rows[:, 128:256]]
        ends = sided(parts, 0, 1.0)
        sides = split(jnp.concatenate([sided(parts, a, 1.0) for a in (1, 2)], axis=1), 0)
        total = dot(sides, jnp.concatenate([inject[0:128], inject[256:384]], axis=0))
        for c in range(3):
            for t in range(4):
                cols = slice(128 * t, 128 * t + 128)
                value = back[c, :, cols] + (total[64 * c:64 * c + 64, cols] + total[192 + 64 * c:256 + 64 * c, cols])
                if t in (0, 3):
                    value = value + at_ends(ends[64 * c:64 * c + 64], t)
                out_ref[c, :, cols] = value * coef[2]

    loads[0].start()
    loads[1].start()
    barrier = pltpu.get_barrier_semaphore()
    for q in OTHERS:
        guarded(q, lambda q=q: pl.semaphore_signal(barrier, inc=1, device_id=device(q), device_id_type=MESH))
    for load in loads[2:]:
        load.start()
    pl.when(jnp.logical_not(has_across))(clear)
    slot = request()
    pl.semaphore_wait(barrier, present)
    for q in OTHERS:
        send(q, lists, lists_in, list_ssem, list_rsem, 1)
    lists_in[SELF] = lists[SELF]
    prepare(slot)

    for batch in F_BATCHES:
        for q in batch:
            if q != SELF:
                arrive(q, lists_in, list_ssem, list_rsem, 1)
        gather(batch)
        for q in batch:
            if q != SELF:
                send(q, fsend, frecv, f_ssem, f_rsem)

    loaded(10, 11)
    lax.fori_loop(0, 8, inner, 0)
    for i in range(3):
        selection(i)
    loaded(11, 14)
    for n, i in enumerate((1, 0, 2)):
        for q in range(4 * i, 4 * i + 4):
            if q != SELF:
                arrive(q, frecv, f_ssem, f_rsem)
        collect(i, place_t, frecv, n == 0)
    ghosts()
    lax.fori_loop(0, 4, stress, 0)
    adjoint_faces()
    for batch in A_BATCHES:
        scatter(batch)
        for q in batch:
            if q != SELF:
                send(q, asend, arecv, a_ssem, a_rsem)

    lax.fori_loop(0, 8, outer, 0)
    for n, i in enumerate((0, 1, 2)):
        for q in range(4 * i, 4 * i + 4):
            if q != SELF:
                arrive(q, arecv, a_ssem, a_rsem)
        collect(i, sel_t, arecv, n == 0)
    land()
    for q, copy in sends:
        guarded(q, copy.wait_send)


def per_device(
    direction, jacobian, shear_modulus, lame_modulus, refine_level, live_flag, neighbor, face_kind, face_quadrant
):
    ranges = lax.axis_size("morton")
    operands = [
        jnp.transpose(direction, (1, 0, 2)),
        jacobian,
        shear_modulus[None, :],
        lame_modulus[None, :],
        refine_level[None, :],
        live_flag[None, :],
        neighbor.T,
        face_kind.T,
        face_quadrant.T,
    ] + tables()
    buffers = [pltpu.VMEM(o.shape, o.dtype) for o in operands]
    operands = [pltpu.with_memory_space_constraint(o, pltpu.HBM) for o in operands]
    message = pltpu.VMEM((PEERS, 96, 128), F32)
    short = pltpu.VMEM((PEERS, 8, 128), F32)
    peers = pltpu.SemaphoreType.DMA((PEERS,))
    result = pl.pallas_call(
        functools.partial(kernel, ranges),
        out_shape=jax.ShapeDtypeStruct((3, BLOCKS, 512), F32),
        in_specs=[pl.BlockSpec(memory_space=pltpu.HBM)] * len(operands),
        out_specs=pl.BlockSpec(memory_space=pltpu.VMEM),
        scratch_shapes=buffers
        + [
            pltpu.VMEM((8, 128), F32),
            pltpu.VMEM((ROWS, 128), F32),
            pltpu.VMEM((3, 64, 128), F32),
            pltpu.VMEM((2 * ROWS, 256), BF16),
            pltpu.VMEM((3, ROWS, 512), BF16),
            pltpu.VMEM((SLOTS, ROWS), BF16),
            pltpu.VMEM((3, ROWS, 512), BF16),
            short,
            short,
            message,
            message,
            message,
            message,
            pltpu.VMEM((ROWS, 256), F32),
            pltpu.VMEM((2 * ROWS, 256), BF16),
            pltpu.VMEM((6, 64, 512), F32),
            pltpu.VMEM((2, 5, 64, 512), BF16),
            pltpu.VMEM((3, 64, 128), F32),
            pltpu.VMEM((2, 3, 64, 512), F32),
            pltpu.VMEM((3, 64, 512), F32),
            pltpu.SemaphoreType.DMA((len(operands),)),
            peers,
            peers,
            peers,
            peers,
            peers,
            peers,
        ],
        compiler_params=pltpu.CompilerParams(
            collective_id=0, has_side_effects=True, vmem_limit_bytes=48 * 1024 * 1024
        ),
        name="hessian_exchange",
    )(*operands)
    return jnp.transpose(result, (1, 0, 2))


def solution(mesh):
    in_specs = (
        P(("morton", "sub"), None, None),
        P(("morton", "sub"), None),
        P(("morton", "sub")),
        P(("morton", "sub")),
        P(("morton", "sub")),
        P(("morton", "sub")),
        P(("morton", "sub"), None),
        P(("morton", "sub"), None),
        P(("morton", "sub"), None),
    )
    out_specs = P(("morton", "sub"), None, None)
    return jax.shard_map(
        per_device, mesh=mesh, in_specs=in_specs, out_specs=out_specs, check_vma=False
    )
```

```python
import functools

import jax
import jax.numpy as jnp
import numpy as np
from jax import lax
from jax.experimental import pallas as pl
from jax.experimental.pallas import tpu as pltpu
from jax.sharding import PartitionSpec as P

BLOCKS = 64
ROWS = 6 * BLOCKS
PEERS = 12
SLOTS = PEERS * BLOCKS
F32 = jnp.float32
BF16 = jnp.bfloat16
MESH = pl.DeviceIdType.MESH
STEPS = (2, 1, 3, 0)
SELF = 7
OTHERS = tuple(q for q in range(PEERS) if q != SELF)
F_BATCHES = ((5, 6), (4, 7), (8, 9, 10, 11), (0, 1, 2, 3))
A_BATCHES = ((0, 1), (2, 3), (8, 9, 10, 11), (4, 5, 6, 7))
PAIRS = {(0, 0): 0, (1, 1): 1, (2, 2): 2, (0, 1): 3, (0, 2): 4, (1, 2): 5}


def pair(a, b):
    return PAIRS[(min(a, b), max(a, b))]


def mirror(q):
    return q - q % 4 + STEPS.index((4 - STEPS[q % 4]) % 4)


def tables():
    node = np.arange(512)
    coords = (node // 64, (node // 8) % 8, node % 8)
    pick = np.zeros((512, 6, 64), np.float32)
    for face in range(6):
        axis = face // 2
        others = [coords[a] for a in range(3) if a != axis]
        for n in np.nonzero(coords[axis] == 7 * (face % 2))[0]:
            pick[n, face, others[0][n] * 8 + others[1][n]] = 1
    halves = np.zeros((2, 8, 8), np.float32)
    for u in range(2):
        for i in range(8):
            halves[u, i, (7 * u + i) // 2] += 0.5
            halves[u, i, (7 * u + i + 1) // 2] += 0.5
    fill = np.zeros((128, 512), np.float32)
    unfill = np.zeros((128, 512), np.float32)
    for q in range(4):
        spread = np.kron(halves[q // 2], halves[q % 2])
        for half in range(2):
            lanes = slice(64 * half, 64 * half + 64)
            cols = slice(128 * q + 64 * half, 128 * q + 64 * half + 64)
            fill[lanes, cols] = spread.T
            unfill[lanes, cols] = spread
    twice = np.concatenate([pick, pick], axis=2).reshape(512, 768)
    inject = pick.reshape(512, 3, 128).transpose(1, 2, 0)[1:]
    inject = np.concatenate([inject, inject], axis=1).reshape(512, 512)
    before = np.triu(np.ones((ROWS, ROWS), np.float32), 1)
    stacked = (np.concatenate([t, t], axis=0) for t in (fill, unfill))
    return [jnp.asarray(t, BF16) for t in (twice, inject, *stacked, before)]


def split(values, axis):
    high = values.astype(BF16)
    low = (values - high.astype(F32)).astype(BF16)
    return jnp.concatenate([high, low], axis=axis)


def dot(a, b):
    return jnp.dot(a, b, preferred_element_type=F32)


def lane_iota(shape):
    return lax.broadcasted_iota(jnp.int32, shape, len(shape) - 1)


def row_iota(shape):
    return lax.broadcasted_iota(jnp.int32, shape, 0)


def one_hot(hits):
    return hits.astype(F32).astype(BF16)


def kernel(
    ranges,
    x_hbm, jac_hbm, mu_hbm, lam_hbm, level_hbm, live_hbm, nb_hbm, kind_hbm, quad_hbm,
    twice_hbm, inject_hbm, fill_hbm, unfill_hbm, before_hbm,
    out_ref,
    x, jac, mu, lam, level, live, nb, kind, quad,
    twice, inject, fill, unfill, before,
    tile_s, code_b, coef, table, sel_t, place, place_t, lists, lists_in,
    fsend, frecv, asend, arecv, gathered, leaving, sym, terms, edge, inj, back,
    in_sem, list_ssem, list_rsem, f_ssem, f_rsem, a_ssem, a_rsem,
):
    me_m = lax.axis_index("morton")
    me_x = lax.axis_index("sub")
    across = lax.rem(me_m, 2) * 2 - 1
    has_across = jnp.logical_and(me_m > 0, me_m < ranges - 1)
    present = 7 + 4 * has_across.astype(jnp.int32)
    low_half = lane_iota((1, 128)) < 64

    def device(q):
        return (me_m + across * (1 - q // 4), lax.rem(me_x + STEPS[q % 4], 4))

    def guarded(q, act):
        if q // 4 == 0:
            pl.when(has_across)(act)
        else:
            act()

    sends = []

    def send(q, src, dst, ssem, rsem, rows=96):
        copy = pltpu.make_async_remote_copy(
            src_ref=src.at[q, 0:rows], dst_ref=dst.at[mirror(q), 0:rows], send_sem=ssem.at[q], recv_sem=rsem.at[mirror(q)],
            device_id=device(q), device_id_type=MESH,
        )
        guarded(q, copy.start)
        sends.append((q, copy))

    def arrive(q, dst, ssem, rsem, rows=96):
        copy = pltpu.make_async_remote_copy(
            src_ref=dst.at[q, 0:rows], dst_ref=dst.at[q, 0:rows], send_sem=ssem.at[q], recv_sem=rsem.at[q],
            device_id=device(q), device_id_type=MESH,
        )
        guarded(q, copy.wait_recv)

    loads = [
        pltpu.make_async_copy(src, dst, in_sem.at[i])
        for i, (src, dst) in enumerate(
            (
                (nb_hbm, nb), (before_hbm, before), (kind_hbm, kind), (quad_hbm, quad),
                (live_hbm, live), (mu_hbm, mu), (lam_hbm, lam), (level_hbm, level),
                (x_hbm, x), (twice_hbm, twice), (jac_hbm, jac), (inject_hbm, inject),
                (fill_hbm, fill), (unfill_hbm, unfill),
            )
        )
    ]

    def loaded(first, last):
        for load in loads[first:last]:
            load.wait()

    def clear():
        for q in range(4):
            frecv[q] = jnp.zeros((96, 128), F32)
            arecv[q] = jnp.zeros((96, 128), F32)
            lists_in[q] = jnp.zeros((8, 128), F32)

    def request():
        loaded(0, 2)
        tile_s[...] = jnp.zeros((8, 128), F32)
        want = nb[...]
        owner = want >> 6
        step = (owner - me_x) & 3
        place_of = jnp.where(step == 2, 0, jnp.where(step == 0, 3, jnp.where(step == 1, 1, 2)))
        peer = (1 - across * ((owner >> 2) - me_m)) * 4 + place_of
        opposite = row_iota((6, 64)) ^ 1
        tile_s[0:6, 0:64] = (peer * 512 + opposite * 64 + (want & 63)).astype(F32)
        packed = tile_s[...]
        turned = pltpu.roll(packed, 64, axis=1)
        pairs = [jnp.where(low_half, packed[f:f + 1], turned[f + 1:f + 2]) for f in (0, 2, 4)]
        row = jnp.concatenate(pairs, axis=1).astype(jnp.int32)
        ident = row & 511
        hits = row_iota((16, ROWS)) == (row >> 9)
        rank = dot(one_hot(hits), before[...])
        base = (row_iota((16, ROWS)) * 64).astype(F32)
        slot = jnp.sum(jnp.where(hits, rank + base, 0.0), axis=0, keepdims=True)
        place[...] = one_hot(row_iota((SLOTS, ROWS)).astype(F32) == slot)
        which = row_iota((8, ROWS))
        parts = jnp.where(which == 0, ident & 63, jnp.where(which == 1, ident >> 6, 0))
        found = lax.dot_general(
            parts.astype(F32).astype(BF16), place[...], (((1,), (1,)), ((), ())), preferred_element_type=F32
        )
        codes = jnp.broadcast_to(found[0:1] + 64.0 * found[1:2], (8, SLOTS))
        for t in range(PEERS // 2):
            both = codes[:, 128 * t:128 * t + 128]
            swapped = pltpu.roll(both, 64, axis=1)
            lists[2 * t] = jnp.where(low_half, both, swapped)
            lists[2 * t + 1] = jnp.where(low_half, swapped, both)
        return slot

    def prepare(slot):
        slot_col = jnp.broadcast_to(slot, (8, ROWS)).T[:, 0:1]
        lanes = (lane_iota((ROWS, 512)) & 255).astype(F32)
        for i in range(3):
            place_t[i] = one_hot(lanes == slot_col - 256.0 * i)
        loaded(2, 8)
        scale = jnp.left_shift(jnp.ones((1, 64), jnp.int32), level[...]).astype(F32) * 0.25
        tile_s[...] = jnp.zeros((8, 128), F32)
        tile_s[0:1, 0:64] = lam[...] * scale * scale
        tile_s[1:2, 0:64] = mu[...] * scale * scale
        tile_s[2:3, 0:64] = live[...].astype(F32)
        flat = tile_s[...].T
        for i in range(3):
            coef[i] = jnp.broadcast_to(flat[0:64, i:i + 1], (64, 128))
        tile_s[...] = jnp.zeros((8, 128), F32)
        kinds = kind[...]
        tile_s[0:6, 0:64] = jnp.where(kinds == 1, 4, jnp.where(kinds == 2, quad[...], -1)).astype(F32)
        flat = tile_s[...].T
        for f in range(6):
            code_b[64 * f:64 * f + 64] = jnp.broadcast_to(flat[0:64, f:f + 1], (64, 128))
        loaded(8, 9)
        alive = jnp.concatenate([coef[2]] * 4, axis=1)
        for c in range(3):
            x[c] = x[c] * alive
        loaded(9, 10)
        parts = split(x[...].reshape(192, 512), 0)
        layers = dot(parts, twice[...])
        for i in range(2):
            for f in range(6):
                cut = layers[192 * i:192 * i + 192, 128 * f:128 * f + 128]
                rows = slice(ROWS * i + 64 * f, ROWS * i + 64 * f + 64)
                table[rows, 0:128] = jnp.where(low_half, cut[0:64], cut[64:128]).astype(BF16)
                table[rows, 128:256] = cut[128:192].astype(BF16)

    def pack(buffer, q, rows):
        buffer[q, 0:64] = rows[:, 0:128]
        buffer[q, 64:96] = jnp.where(low_half, rows[0:32, 128:256], rows[32:64, 128:256])

    def unpack(message):
        tail = message[64:96]
        other = pltpu.roll(tail, 64, axis=1)
        third = jnp.concatenate([jnp.where(low_half, tail, other), jnp.where(low_half, other, tail)], axis=0)
        return jnp.concatenate([message[0:64], third], axis=1)

    def gather(batch):
        lane_row = lane_iota((64, ROWS)).astype(F32)
        chosen = []
        for q in batch:
            column = jnp.broadcast_to(lists_in[q, 0:1], (8, 128)).T[0:64, 0:1]
            chosen.append(one_hot(lane_row == column))
        chosen = jnp.concatenate(chosen, axis=0)
        rows = dot(jnp.concatenate([chosen, chosen], axis=1), table[...])
        for n, q in enumerate(batch):
            pack(frecv if q == SELF else fsend, q, rows[64 * n:64 * n + 64])

    def selection(i):
        a, b, c, d = (lists_in[q, 0:1] for q in range(4 * i, 4 * i + 4))
        ids = [jnp.where(low_half, a, b), jnp.where(low_half, c, d)] * 2
        sel_t[i] = one_hot(row_iota((ROWS, 512)).astype(F32) == jnp.concatenate(ids, axis=1))

    def collect(i, weights, messages, first):
        rows = jnp.concatenate([unpack(messages[q]) for q in range(4 * i, 4 * i + 4)], axis=0)
        part = dot(weights[i], split(rows, 0))
        gathered[...] = part if first else gathered[...] + part

    lane = lane_iota((1, 128))
    ok_up2, ok_dn2 = (lane & 7) < 7, (lane & 7) > 0
    ok_up1, ok_dn1 = (lane & 63) < 56, (lane & 63) >= 8

    def step2(v):
        return jnp.where(ok_up2, pltpu.roll(v, 127, axis=1), 0.0) - jnp.where(ok_dn2, pltpu.roll(v, 1, axis=1), 0.0)

    def step1(v):
        return jnp.where(ok_up1, pltpu.roll(v, 120, axis=1), 0.0) - jnp.where(ok_dn1, pltpu.roll(v, 8, axis=1), 0.0)

    def step0(tiles):
        swung = [pltpu.roll(v, 64, axis=1) for v in tiles]
        none = jnp.zeros_like(swung[0])
        up = [jnp.where(low_half, swung[t], swung[t + 1] if t < 3 else none) for t in range(4)]
        dn = [jnp.where(low_half, swung[t - 1] if t > 0 else none, swung[t]) for t in range(4)]
        return [u - d for u, d in zip(up, dn)]

    def inner(i, _):
        rows = pl.ds(pl.multiple_of(i * 8, 8), 8)
        tiles = [[x[c, rows, 128 * t:128 * t + 128] for t in range(4)] for c in range(3)]
        first = [step0(tiles[c]) for c in range(3)]
        for t in range(4):
            cols = slice(128 * t, 128 * t + 128)
            d = [[first[c][t], step1(tiles[c][t]), step2(tiles[c][t])] for c in range(3)]
            for a in range(3):
                sym[a, rows, cols] = d[a][a]
                for b in range(a + 1, 3):
                    sym[pair(a, b), rows, cols] = d[a][b] + d[b][a]
            jac[rows, cols] = coef[1, rows] - coef[0, rows] * jnp.log(jac[rows, cols])
        return 0

    def by_quadrant(parts, weights):
        code = code_b[...]
        masks = [code == float(q) for q in range(5)]
        result = []
        for half in range(2):
            cut = slice(128 * half, 128 * half + 128)
            value = parts[:, cut]
            spread = dot(split(value, 1), weights[...])
            value = jnp.where(masks[4], value, 0.0)
            for q in range(4):
                value = jnp.where(masks[q], spread[:, 128 * q:128 * q + 128], value)
            result.append(value)
        return result

    def sided(parts, a, sign):
        low = [sign * part[128 * a:128 * a + 64] for part in parts]
        high = [part[128 * a + 64:128 * a + 128] for part in parts]
        return jnp.concatenate(
            [
                jnp.where(low_half, low[0], pltpu.roll(high[0], 64, axis=1)),
                jnp.where(low_half, pltpu.roll(low[0], 64, axis=1), high[0]),
                jnp.where(low_half, low[1], high[1]),
            ],
            axis=0,
        )

    def ghosts():
        parts = by_quadrant(gathered[...], fill)
        edge[...] = sided(parts, 0, -1.0).reshape(3, 64, 128)
        for a in (1, 2):
            sides = split(sided(parts, a, -1.0), 1)
            inj[a - 1] = dot(sides, inject[256 * a - 256:256 * a]).reshape(3, 64, 512)

    def at_ends(v, t):
        return jnp.where(low_half, v, 0.0) if t == 0 else jnp.where(low_half, 0.0, v)

    def stress(i, _):
        rows = pl.ds(pl.multiple_of(i * 16, 16), 16)
        for t in range(4):
            cols = slice(128 * t, 128 * t + 128)
            shear = jac[rows, cols]
            e = [sym[k, rows, cols] for k in range(6)]
            if t in (0, 3):
                for c in range(3):
                    e[pair(c, 0)] = e[pair(c, 0)] + at_ends(edge[c, rows], t)
            for a in (1, 2):
                for c in range(3):
                    e[pair(c, a)] = e[pair(c, a)] + inj[a - 1, c, rows, cols]
            trace = coef[0, rows] * (e[0] + e[1] + e[2])
            for k in range(6):
                value = trace + 2.0 * shear * e[k] if k < 3 else shear * e[k]
                sym[k, rows, cols] = value
                if k > 0:
                    high = value.astype(BF16)
                    terms[0, k - 1, rows, cols] = high
                    terms[1, k - 1, rows, cols] = (value - high.astype(F32)).astype(BF16)
        return 0

    def adjoint_faces():
        first = [sym[pair(c, 0), :, 0:128] for c in range(3)]
        last = [sym[pair(c, 0), :, 384:512] for c in range(3)]

        def swing(v):
            return pltpu.roll(v, 64, axis=1)

        bars = [
            jnp.concatenate(
                [-jnp.where(low_half, first[0], swing(first[1])), -jnp.where(low_half, first[2], swing(first[2]))], axis=1
            ),
            jnp.concatenate(
                [jnp.where(low_half, swing(last[0]), last[1]), jnp.where(low_half, swing(last[2]), last[2])], axis=1
            ),
        ]
        for a in (1, 2):
            stacked = [terms[part, pair(c, a) - 1] for part in range(2) for c in range(3)]
            layers = dot(jnp.concatenate(stacked, axis=0), twice[:, 256 * a:256 * a + 256])
            layers = layers[0:192] + layers[192:384]
            for side in range(2):
                cut = layers[:, 128 * side:128 * side + 128]
                if side == 0:
                    cut = -cut
                bars.append(jnp.concatenate([jnp.where(low_half, cut[0:64], cut[64:128]), cut[128:192]], axis=1))
        parts = by_quadrant(jnp.concatenate(bars, axis=0), unfill)
        leaving[...] = split(jnp.concatenate(parts, axis=1), 0)

    def scatter(batch):
        chosen = place[64 * batch[0]:64 * batch[-1] + 64]
        rows = dot(jnp.concatenate([chosen, chosen], axis=1), leaving[...])
        for n, q in enumerate(batch):
            pack(arecv if q == SELF else asend, q, rows[64 * n:64 * n + 64])

    def outer(i, _):
        rows = pl.ds(pl.multiple_of(i * 8, 8), 8)
        for c in range(3):
            first = step0([sym[pair(c, 0), rows, 128 * t:128 * t + 128] for t in range(4)])
            for t in range(4):
                cols = slice(128 * t, 128 * t + 128)
                back[c, rows, cols] = -(
                    first[t] + step1(sym[pair(c, 1), rows, cols]) + step2(sym[pair(c, 2), rows, cols])
                )
        return 0

    def land():
        rows = gathered[...]
        parts = [rows[:, 0:128], rows[:, 128:256]]
        ends = sided(parts, 0, 1.0)
        sides = split(jnp.concatenate([sided(parts, a, 1.0) for a in (1, 2)], axis=1), 0)
        total = dot(sides, jnp.concatenate([inject[0:128], inject[256:384]], axis=0))
        for c in range(3):
            for t in range(4):
                cols = slice(128 * t, 128 * t + 128)
                value = back[c, :, cols] + (total[64 * c:64 * c + 64, cols] + total[192 + 64 * c:256 + 64 * c, cols])
                if t in (0, 3):
                    value = value + at_ends(ends[64 * c:64 * c + 64], t)
                out_ref[c, :, cols] = value * coef[2]

    loads[0].start()
    loads[1].start()
    barrier = pltpu.get_barrier_semaphore()
    for q in OTHERS:
        guarded(q, lambda q=q: pl.semaphore_signal(barrier, inc=1, device_id=device(q), device_id_type=MESH))
    for load in loads[2:]:
        load.start()
    pl.when(jnp.logical_not(has_across))(clear)
    slot = request()
    pl.semaphore_wait(barrier, present)
    for q in OTHERS:
        send(q, lists, lists_in, list_ssem, list_rsem, 1)
    lists_in[SELF] = lists[SELF]
    prepare(slot)

    for batch in F_BATCHES:
        for q in batch:
            if q != SELF:
                arrive(q, lists_in, list_ssem, list_rsem, 1)
        gather(batch)
        for q in batch:
            if q != SELF:
                send(q, fsend, frecv, f_ssem, f_rsem)

    loaded(10, 11)
    lax.fori_loop(0, 8, inner, 0)
    for i in range(3):
        selection(i)
    loaded(11, 14)
    for n, i in enumerate((1, 2, 0)):
        for q in range(4 * i, 4 * i + 4):
            if q != SELF:
                arrive(q, frecv, f_ssem, f_rsem)
        collect(i, place_t, frecv, n == 0)
    ghosts()
    lax.fori_loop(0, 4, stress, 0)
    adjoint_faces()
    for batch in A_BATCHES:
        scatter(batch)
        for q in batch:
            if q != SELF:
                send(q, asend, arecv, a_ssem, a_rsem)

    lax.fori_loop(0, 8, outer, 0)
    for n, i in enumerate((0, 2, 1)):
        for q in range(4 * i, 4 * i + 4):
            if q != SELF:
                arrive(q, arecv, a_ssem, a_rsem)
        collect(i, sel_t, arecv, n == 0)
    land()
    for q, copy in sends:
        guarded(q, copy.wait_send)


def per_device(
    direction, jacobian, shear_modulus, lame_modulus, refine_level, live_flag, neighbor, face_kind, face_quadrant
):
    ranges = lax.axis_size("morton")
    operands = [
        jnp.transpose(direction, (1, 0, 2)),
        jacobian,
        shear_modulus[None, :],
        lame_modulus[None, :],
        refine_level[None, :],
        live_flag[None, :],
        neighbor.T,
        face_kind.T,
        face_quadrant.T,
    ] + tables()
    buffers = [pltpu.VMEM(o.shape, o.dtype) for o in operands]
    operands = [pltpu.with_memory_space_constraint(o, pltpu.HBM) for o in operands]
    message = pltpu.VMEM((PEERS, 96, 128), F32)
    short = pltpu.VMEM((PEERS, 8, 128), F32)
    peers = pltpu.SemaphoreType.DMA((PEERS,))
    result = pl.pallas_call(
        functools.partial(kernel, ranges),
        out_shape=jax.ShapeDtypeStruct((3, BLOCKS, 512), F32),
        in_specs=[pl.BlockSpec(memory_space=pltpu.HBM)] * len(operands),
        out_specs=pl.BlockSpec(memory_space=pltpu.VMEM),
        scratch_shapes=buffers
        + [
            pltpu.VMEM((8, 128), F32),
            pltpu.VMEM((ROWS, 128), F32),
            pltpu.VMEM((3, 64, 128), F32),
            pltpu.VMEM((2 * ROWS, 256), BF16),
            pltpu.VMEM((3, ROWS, 512), BF16),
            pltpu.VMEM((SLOTS, ROWS), BF16),
            pltpu.VMEM((3, ROWS, 512), BF16),
            short,
            short,
            message,
            message,
            message,
            message,
            pltpu.VMEM((ROWS, 256), F32),
            pltpu.VMEM((2 * ROWS, 256), BF16),
            pltpu.VMEM((6, 64, 512), F32),
            pltpu.VMEM((2, 5, 64, 512), BF16),
            pltpu.VMEM((3, 64, 128), F32),
            pltpu.VMEM((2, 3, 64, 512), F32),
            pltpu.VMEM((3, 64, 512), F32),
            pltpu.SemaphoreType.DMA((len(operands),)),
            peers,
            peers,
            peers,
            peers,
            peers,
            peers,
        ],
        compiler_params=pltpu.CompilerParams(
            collective_id=0, has_side_effects=True, vmem_limit_bytes=48 * 1024 * 1024
        ),
        name="hessian_exchange",
    )(*operands)
    return jnp.transpose(result, (1, 0, 2))


def solution(mesh):
    in_specs = (
        P(("morton", "sub"), None, None),
        P(("morton", "sub"), None),
        P(("morton", "sub")),
        P(("morton", "sub")),
        P(("morton", "sub")),
        P(("morton", "sub")),
        P(("morton", "sub"), None),
        P(("morton", "sub"), None),
        P(("morton", "sub"), None),
    )
    out_specs = P(("morton", "sub"), None, None)
    return jax.shard_map(
        per_device, mesh=mesh, in_specs=in_specs, out_specs=out_specs, check_vma=False
    )
```

```python
import functools

import jax
import jax.numpy as jnp
import numpy as np
from jax import lax
from jax.experimental import pallas as pl
from jax.experimental.pallas import tpu as pltpu
from jax.sharding import PartitionSpec as P

BLOCKS = 64
ROWS = 6 * BLOCKS
PEERS = 12
SLOTS = PEERS * BLOCKS
F32 = jnp.float32
BF16 = jnp.bfloat16
MESH = pl.DeviceIdType.MESH
STEPS = (2, 1, 3, 0)
SELF = 7
OTHERS = tuple(q for q in range(PEERS) if q != SELF)
F_BATCHES = ((5, 6), (4, 7), (8, 9, 10, 11), (0, 1, 2, 3))
A_BATCHES = ((0, 1), (2, 3), (8, 9, 10, 11), (4, 5, 6, 7))
PAIRS = {(0, 0): 0, (1, 1): 1, (2, 2): 2, (0, 1): 3, (0, 2): 4, (1, 2): 5}


def pair(a, b):
    return PAIRS[(min(a, b), max(a, b))]


def mirror(q):
    return q - q % 4 + STEPS.index((4 - STEPS[q % 4]) % 4)


def tables():
    node = np.arange(512)
    coords = (node // 64, (node // 8) % 8, node % 8)
    pick = np.zeros((512, 6, 64), np.float32)
    for face in range(6):
        axis = face // 2
        others = [coords[a] for a in range(3) if a != axis]
        for n in np.nonzero(coords[axis] == 7 * (face % 2))[0]:
            pick[n, face, others[0][n] * 8 + others[1][n]] = 1
    halves = np.zeros((2, 8, 8), np.float32)
    for u in range(2):
        for i in range(8):
            halves[u, i, (7 * u + i) // 2] += 0.5
            halves[u, i, (7 * u + i + 1) // 2] += 0.5
    fill = np.zeros((128, 512), np.float32)
    unfill = np.zeros((128, 512), np.float32)
    for q in range(4):
        spread = np.kron(halves[q // 2], halves[q % 2])
        for half in range(2):
            lanes = slice(64 * half, 64 * half + 64)
            cols = slice(128 * q + 64 * half, 128 * q + 64 * half + 64)
            fill[lanes, cols] = spread.T
            unfill[lanes, cols] = spread
    twice = np.concatenate([pick, pick], axis=2).reshape(512, 768)
    inject = pick.reshape(512, 3, 128).transpose(1, 2, 0)[1:]
    inject = np.concatenate([inject, inject], axis=1).reshape(512, 512)
    before = np.triu(np.ones((ROWS, ROWS), np.float32), 1)
    stacked = (np.concatenate([t, t], axis=0) for t in (fill, unfill))
    return [jnp.asarray(t, BF16) for t in (twice, inject, *stacked, before)]


def split(values, axis):
    high = values.astype(BF16)
    low = (values - high.astype(F32)).astype(BF16)
    return jnp.concatenate([high, low], axis=axis)


def dot(a, b):
    return jnp.dot(a, b, preferred_element_type=F32)


def lane_iota(shape):
    return lax.broadcasted_iota(jnp.int32, shape, len(shape) - 1)


def row_iota(shape):
    return lax.broadcasted_iota(jnp.int32, shape, 0)


def one_hot(hits):
    return hits.astype(F32).astype(BF16)


def kernel(
    ranges,
    x_hbm, jac_hbm, mu_hbm, lam_hbm, level_hbm, live_hbm, nb_hbm, kind_hbm, quad_hbm,
    twice_hbm, inject_hbm, fill_hbm, unfill_hbm, before_hbm,
    out_ref,
    x, jac, mu, lam, level, live, nb, kind, quad,
    twice, inject, fill, unfill, before,
    tile_s, code_b, coef, table, sel_t, place, place_t, lists, lists_in,
    fsend, frecv, asend, arecv, gathered, leaving, sym, terms, edge, inj, back,
    in_sem, list_ssem, list_rsem, f_ssem, f_rsem, a_ssem, a_rsem,
):
    me_m = lax.axis_index("morton")
    me_x = lax.axis_index("sub")
    across = lax.rem(me_m, 2) * 2 - 1
    has_across = jnp.logical_and(me_m > 0, me_m < ranges - 1)
    present = 7 + 4 * has_across.astype(jnp.int32)
    low_half = lane_iota((1, 128)) < 64

    def device(q):
        return (me_m + across * (1 - q // 4), lax.rem(me_x + STEPS[q % 4], 4))

    def guarded(q, act):
        if q // 4 == 0:
            pl.when(has_across)(act)
        else:
            act()

    sends = []

    def send(q, src, dst, ssem, rsem, rows=96):
        copy = pltpu.make_async_remote_copy(
            src_ref=src.at[q, 0:rows], dst_ref=dst.at[mirror(q), 0:rows], send_sem=ssem.at[q], recv_sem=rsem.at[mirror(q)],
            device_id=device(q), device_id_type=MESH,
        )
        guarded(q, copy.start)
        sends.append((q, copy))

    def arrive(q, dst, ssem, rsem, rows=96):
        copy = pltpu.make_async_remote_copy(
            src_ref=dst.at[q, 0:rows], dst_ref=dst.at[q, 0:rows], send_sem=ssem.at[q], recv_sem=rsem.at[q],
            device_id=device(q), device_id_type=MESH,
        )
        guarded(q, copy.wait_recv)

    loads = [
        pltpu.make_async_copy(src, dst, in_sem.at[i])
        for i, (src, dst) in enumerate(
            (
                (nb_hbm, nb), (before_hbm, before), (kind_hbm, kind), (quad_hbm, quad),
                (live_hbm, live), (mu_hbm, mu), (lam_hbm, lam), (level_hbm, level),
                (x_hbm, x), (twice_hbm, twice), (jac_hbm, jac), (inject_hbm, inject),
                (fill_hbm, fill), (unfill_hbm, unfill),
            )
        )
    ]

    def loaded(first, last):
        for load in loads[first:last]:
            load.wait()

    def clear():
        for q in range(4):
            frecv[q] = jnp.zeros((96, 128), F32)
            arecv[q] = jnp.zeros((96, 128), F32)
            lists_in[q] = jnp.zeros((8, 128), F32)

    def request():
        loaded(0, 2)
        tile_s[...] = jnp.zeros((8, 128), F32)
        want = nb[...]
        owner = want >> 6
        step = (owner - me_x) & 3
        place_of = jnp.where(step == 2, 0, jnp.where(step == 0, 3, jnp.where(step == 1, 1, 2)))
        peer = (1 - across * ((owner >> 2) - me_m)) * 4 + place_of
        opposite = row_iota((6, 64)) ^ 1
        tile_s[0:6, 0:64] = (peer * 512 + opposite * 64 + (want & 63)).astype(F32)
        packed = tile_s[...]
        turned = pltpu.roll(packed, 64, axis=1)
        pairs = [jnp.where(low_half, packed[f:f + 1], turned[f + 1:f + 2]) for f in (0, 2, 4)]
        row = jnp.concatenate(pairs, axis=1).astype(jnp.int32)
        ident = row & 511
        hits = row_iota((16, ROWS)) == (row >> 9)
        rank = dot(one_hot(hits), before[...])
        base = (row_iota((16, ROWS)) * 64).astype(F32)
        slot = jnp.sum(jnp.where(hits, rank + base, 0.0), axis=0, keepdims=True)
        place[...] = one_hot(row_iota((SLOTS, ROWS)).astype(F32) == slot)
        which = row_iota((8, ROWS))
        parts = jnp.where(which == 0, ident & 63, jnp.where(which == 1, ident >> 6, 0))
        found = lax.dot_general(
            parts.astype(F32).astype(BF16), place[...], (((1,), (1,)), ((), ())), preferred_element_type=F32
        )
        codes = jnp.broadcast_to(found[0:1] + 64.0 * found[1:2], (8, SLOTS))
        for t in range(PEERS // 2):
            both = codes[:, 128 * t:128 * t + 128]
            swapped = pltpu.roll(both, 64, axis=1)
            lists[2 * t] = jnp.where(low_half, both, swapped)
            lists[2 * t + 1] = jnp.where(low_half, swapped, both)
        return slot

    def prepare(slot):
        slot_col = jnp.broadcast_to(slot, (8, ROWS)).T[:, 0:1]
        lanes = (lane_iota((ROWS, 256)) & 127).astype(F32)
        for i in range(6):
            place_t[i] = one_hot(lanes == slot_col - 128.0 * i)
        loaded(2, 8)
        scale = jnp.left_shift(jnp.ones((1, 64), jnp.int32), level[...]).astype(F32) * 0.25
        tile_s[...] = jnp.zeros((8, 128), F32)
        tile_s[0:1, 0:64] = lam[...] * scale * scale
        tile_s[1:2, 0:64] = mu[...] * scale * scale
        tile_s[2:3, 0:64] = live[...].astype(F32)
        flat = tile_s[...].T
        for i in range(3):
            coef[i] = jnp.broadcast_to(flat[0:64, i:i + 1], (64, 128))
        tile_s[...] = jnp.zeros((8, 128), F32)
        kinds = kind[...]
        tile_s[0:6, 0:64] = jnp.where(kinds == 1, 4, jnp.where(kinds == 2, quad[...], -1)).astype(F32)
        flat = tile_s[...].T
        codes = jnp.concatenate([jnp.broadcast_to(flat[0:64, f:f + 1], (64, 128)) for f in range(6)], axis=0)
        code_b[...] = codes
        loaded(8, 9)
        alive = jnp.concatenate([coef[2]] * 4, axis=1)
        for c in range(3):
            x[c] = x[c] * alive
        loaded(9, 10)
        parts = split(x[...].reshape(192, 512), 0)
        layers = dot(parts, twice[...])
        for i in range(2):
            for f in range(6):
                cut = layers[192 * i:192 * i + 192, 128 * f:128 * f + 128]
                rows = slice(ROWS * i + 64 * f, ROWS * i + 64 * f + 64)
                table[rows, 0:128] = jnp.where(low_half, cut[0:64], cut[64:128]).astype(BF16)
                table[rows, 128:256] = cut[128:192].astype(BF16)

    def pack(buffer, q, rows):
        buffer[q, 0:64] = rows[:, 0:128]
        buffer[q, 64:96] = jnp.where(low_half, rows[0:32, 128:256], rows[32:64, 128:256])

    def unpack(message):
        tail = message[64:96]
        other = pltpu.roll(tail, 64, axis=1)
        third = jnp.concatenate([jnp.where(low_half, tail, other), jnp.where(low_half, other, tail)], axis=0)
        return jnp.concatenate([message[0:64], third], axis=1)

    def gather(batch):
        lane_row = lane_iota((64, ROWS)).astype(F32)
        chosen = []
        for q in batch:
            column = jnp.broadcast_to(lists_in[q, 0:1], (8, 128)).T[0:64, 0:1]
            chosen.append(one_hot(lane_row == column))
        chosen = jnp.concatenate(chosen, axis=0)
        rows = dot(jnp.concatenate([chosen, chosen], axis=1), table[...])
        for n, q in enumerate(batch):
            pack(frecv if q == SELF else fsend, q, rows[64 * n:64 * n + 64])

    def selection(i):
        ids = jnp.where(low_half, lists_in[2 * i, 0:1], lists_in[2 * i + 1, 0:1])
        sel_t[i] = one_hot(row_iota((ROWS, 256)).astype(F32) == jnp.concatenate([ids, ids], axis=1))

    def by_quadrant(rows, weights, code):
        masks = [code == float(q) for q in range(5)]
        result = []
        for half in range(2):
            value = rows[:, 128 * half:128 * half + 128]
            spread = dot(split(value, 1), weights[...])
            value = jnp.where(masks[4], value, 0.0)
            for q in range(4):
                value = jnp.where(masks[q], spread[:, 128 * q:128 * q + 128], value)
            result.append(value)
        return jnp.concatenate(result, axis=1)

    def collect(i, weights, messages, first):
        rows = jnp.concatenate([unpack(messages[2 * i]), unpack(messages[2 * i + 1])], axis=0)
        part = dot(weights[i], split(rows, 0))
        gathered[...] = part if first else gathered[...] + part

    lane = lane_iota((1, 128))
    ok_up2, ok_dn2 = (lane & 7) < 7, (lane & 7) > 0
    ok_up1, ok_dn1 = (lane & 63) < 56, (lane & 63) >= 8

    def step2(v):
        return jnp.where(ok_up2, pltpu.roll(v, 127, axis=1), 0.0) - jnp.where(ok_dn2, pltpu.roll(v, 1, axis=1), 0.0)

    def step1(v):
        return jnp.where(ok_up1, pltpu.roll(v, 120, axis=1), 0.0) - jnp.where(ok_dn1, pltpu.roll(v, 8, axis=1), 0.0)

    def step0(tiles):
        swung = [pltpu.roll(v, 64, axis=1) for v in tiles]
        none = jnp.zeros_like(swung[0])
        up = [jnp.where(low_half, swung[t], swung[t + 1] if t < 3 else none) for t in range(4)]
        dn = [jnp.where(low_half, swung[t - 1] if t > 0 else none, swung[t]) for t in range(4)]
        return [u - d for u, d in zip(up, dn)]

    def inner(i, _):
        rows = pl.ds(pl.multiple_of(i * 8, 8), 8)
        tiles = [[x[c, rows, 128 * t:128 * t + 128] for t in range(4)] for c in range(3)]
        first = [step0(tiles[c]) for c in range(3)]
        for t in range(4):
            cols = slice(128 * t, 128 * t + 128)
            d = [[first[c][t], step1(tiles[c][t]), step2(tiles[c][t])] for c in range(3)]
            for a in range(3):
                sym[a, rows, cols] = d[a][a]
                for b in range(a + 1, 3):
                    sym[pair(a, b), rows, cols] = d[a][b] + d[b][a]
            jac[rows, cols] = coef[1, rows] - coef[0, rows] * jnp.log(jac[rows, cols])
        return 0

    def sided(parts, a, sign):
        low = [sign * part[128 * a:128 * a + 64] for part in parts]
        high = [part[128 * a + 64:128 * a + 128] for part in parts]
        return jnp.concatenate(
            [
                jnp.where(low_half, low[0], pltpu.roll(high[0], 64, axis=1)),
                jnp.where(low_half, pltpu.roll(low[0], 64, axis=1), high[0]),
                jnp.where(low_half, low[1], high[1]),
            ],
            axis=0,
        )

    def ghosts():
        rows = by_quadrant(gathered[...], fill, code_b[...])
        parts = [rows[:, 0:128], rows[:, 128:256]]
        edge[...] = sided(parts, 0, -1.0).reshape(3, 64, 128)
        for a in (1, 2):
            sides = split(sided(parts, a, -1.0), 1)
            inj[a - 1] = dot(sides, inject[256 * a - 256:256 * a]).reshape(3, 64, 512)

    def at_ends(v, t):
        return jnp.where(low_half, v, 0.0) if t == 0 else jnp.where(low_half, 0.0, v)

    def stress(i, _):
        rows = pl.ds(pl.multiple_of(i * 16, 16), 16)
        for t in range(4):
            cols = slice(128 * t, 128 * t + 128)
            shear = jac[rows, cols]
            e = [sym[k, rows, cols] for k in range(6)]
            if t in (0, 3):
                for c in range(3):
                    e[pair(c, 0)] = e[pair(c, 0)] + at_ends(edge[c, rows], t)
            for a in (1, 2):
                for c in range(3):
                    e[pair(c, a)] = e[pair(c, a)] + inj[a - 1, c, rows, cols]
            trace = coef[0, rows] * (e[0] + e[1] + e[2])
            for k in range(6):
                value = trace + 2.0 * shear * e[k] if k < 3 else shear * e[k]
                sym[k, rows, cols] = value
                if k > 0:
                    high = value.astype(BF16)
                    terms[0, k - 1, rows, cols] = high
                    terms[1, k - 1, rows, cols] = (value - high.astype(F32)).astype(BF16)
        return 0

    def adjoint_faces():
        first = [sym[pair(c, 0), :, 0:128] for c in range(3)]
        last = [sym[pair(c, 0), :, 384:512] for c in range(3)]

        def swing(v):
            return pltpu.roll(v, 64, axis=1)

        bars = [
            jnp.concatenate(
                [-jnp.where(low_half, first[0], swing(first[1])), -jnp.where(low_half, first[2], swing(first[2]))], axis=1
            ),
            jnp.concatenate(
                [jnp.where(low_half, swing(last[0]), last[1]), jnp.where(low_half, swing(last[2]), last[2])], axis=1
            ),
        ]
        for a in (1, 2):
            stacked = [terms[part, pair(c, a) - 1] for part in range(2) for c in range(3)]
            layers = dot(jnp.concatenate(stacked, axis=0), twice[:, 256 * a:256 * a + 256])
            layers = layers[0:192] + layers[192:384]
            for side in range(2):
                cut = layers[:, 128 * side:128 * side + 128]
                if side == 0:
                    cut = -cut
                bars.append(jnp.concatenate([jnp.where(low_half, cut[0:64], cut[64:128]), cut[128:192]], axis=1))
        leaving[...] = split(by_quadrant(jnp.concatenate(bars, axis=0), unfill, code_b[...]), 0)

    def scatter(batch):
        slots = slice(64 * batch[0], 64 * batch[-1] + 64)
        chosen = place[slots]
        rows = dot(jnp.concatenate([chosen, chosen], axis=1), leaving[...])
        for n, q in enumerate(batch):
            pack(arecv if q == SELF else asend, q, rows[64 * n:64 * n + 64])

    def outer(i, _):
        rows = pl.ds(pl.multiple_of(i * 8, 8), 8)
        for c in range(3):
            first = step0([sym[pair(c, 0), rows, 128 * t:128 * t + 128] for t in range(4)])
            for t in range(4):
                cols = slice(128 * t, 128 * t + 128)
                back[c, rows, cols] = -(
                    first[t] + step1(sym[pair(c, 1), rows, cols]) + step2(sym[pair(c, 2), rows, cols])
                )
        return 0

    def land():
        rows = gathered[...]
        parts = [rows[:, 0:128], rows[:, 128:256]]
        ends = sided(parts, 0, 1.0)
        sides = split(jnp.concatenate([sided(parts, a, 1.0) for a in (1, 2)], axis=1), 0)
        total = dot(sides, jnp.concatenate([inject[0:128], inject[256:384]], axis=0))
        for c in range(3):
            for t in range(4):
                cols = slice(128 * t, 128 * t + 128)
                value = back[c, :, cols] + (total[64 * c:64 * c + 64, cols] + total[192 + 64 * c:256 + 64 * c, cols])
                if t in (0, 3):
                    value = value + at_ends(ends[64 * c:64 * c + 64], t)
                out_ref[c, :, cols] = value * coef[2]

    loads[0].start()
    loads[1].start()
    barrier = pltpu.get_barrier_semaphore()
    for q in OTHERS:
        guarded(q, lambda q=q: pl.semaphore_signal(barrier, inc=1, device_id=device(q), device_id_type=MESH))
    for load in loads[2:]:
        load.start()
    pl.when(jnp.logical_not(has_across))(clear)
    slot = request()
    pl.semaphore_wait(barrier, present)
    for q in OTHERS:
        send(q, lists, lists_in, list_ssem, list_rsem, 1)
    lists_in[SELF] = lists[SELF]
    prepare(slot)

    for batch in F_BATCHES:
        for q in batch:
            if q != SELF:
                arrive(q, lists_in, list_ssem, list_rsem, 1)
        gather(batch)
        for q in batch:
            if q != SELF:
                send(q, fsend, frecv, f_ssem, f_rsem)

    loaded(10, 11)
    lax.fori_loop(0, 8, inner, 0)
    for i in range(6):
        selection(i)
    loaded(11, 14)
    for n, i in enumerate((2, 3, 4, 5, 0, 1)):
        for q in (2 * i, 2 * i + 1):
            if q != SELF:
                arrive(q, frecv, f_ssem, f_rsem)
        collect(i, place_t, frecv, n == 0)
    ghosts()
    lax.fori_loop(0, 4, stress, 0)
    adjoint_faces()
    for batch in A_BATCHES:
        scatter(batch)
        for q in batch:
            if q != SELF:
                send(q, asend, arecv, a_ssem, a_rsem)

    lax.fori_loop(0, 8, outer, 0)
    for n, i in enumerate((0, 1, 4, 5, 2, 3)):
        for q in (2 * i, 2 * i + 1):
            if q != SELF:
                arrive(q, arecv, a_ssem, a_rsem)
        collect(i, sel_t, arecv, n == 0)
    land()
    for q, copy in sends:
        guarded(q, copy.wait_send)


def per_device(
    direction, jacobian, shear_modulus, lame_modulus, refine_level, live_flag, neighbor, face_kind, face_quadrant
):
    ranges = lax.axis_size("morton")
    operands = [
        jnp.transpose(direction, (1, 0, 2)),
        jacobian,
        shear_modulus[None, :],
        lame_modulus[None, :],
        refine_level[None, :],
        live_flag[None, :],
        neighbor.T,
        face_kind.T,
        face_quadrant.T,
    ] + tables()
    buffers = [pltpu.VMEM(o.shape, o.dtype) for o in operands]
    operands = [pltpu.with_memory_space_constraint(o, pltpu.HBM) for o in operands]
    message = pltpu.VMEM((PEERS, 96, 128), F32)
    short = pltpu.VMEM((PEERS, 8, 128), F32)
    peers = pltpu.SemaphoreType.DMA((PEERS,))
    result = pl.pallas_call(
        functools.partial(kernel, ranges),
        out_shape=jax.ShapeDtypeStruct((3, BLOCKS, 512), F32),
        in_specs=[pl.BlockSpec(memory_space=pltpu.HBM)] * len(operands),
        out_specs=pl.BlockSpec(memory_space=pltpu.VMEM),
        scratch_shapes=buffers
        + [
            pltpu.VMEM((8, 128), F32),
            pltpu.VMEM((ROWS, 128), F32),
            pltpu.VMEM((3, 64, 128), F32),
            pltpu.VMEM((2 * ROWS, 256), BF16),
            pltpu.VMEM((6, ROWS, 256), BF16),
            pltpu.VMEM((SLOTS, ROWS), BF16),
            pltpu.VMEM((6, ROWS, 256), BF16),
            short,
            short,
            message,
            message,
            message,
            message,
            pltpu.VMEM((ROWS, 256), F32),
            pltpu.VMEM((2 * ROWS, 256), BF16),
            pltpu.VMEM((6, 64, 512), F32),
            pltpu.VMEM((2, 5, 64, 512), BF16),
            pltpu.VMEM((3, 64, 128), F32),
            pltpu.VMEM((2, 3, 64, 512), F32),
            pltpu.VMEM((3, 64, 512), F32),
            pltpu.SemaphoreType.DMA((len(operands),)),
            peers,
            peers,
            peers,
            peers,
            peers,
            peers,
        ],
        compiler_params=pltpu.CompilerParams(
            collective_id=0, has_side_effects=True, vmem_limit_bytes=48 * 1024 * 1024
        ),
        name="hessian_exchange",
    )(*operands)
    return jnp.transpose(result, (1, 0, 2))


def solution(mesh):
    in_specs = (
        P(("morton", "sub"), None, None),
        P(("morton", "sub"), None),
        P(("morton", "sub")),
        P(("morton", "sub")),
        P(("morton", "sub")),
        P(("morton", "sub")),
        P(("morton", "sub"), None),
        P(("morton", "sub"), None),
        P(("morton", "sub"), None),
    )
    out_specs = P(("morton", "sub"), None, None)
    return jax.shard_map(
        per_device, mesh=mesh, in_specs=in_specs, out_specs=out_specs, check_vma=False
    )
```
